256 devices in a mesh: tm: 4 (over z_hi), height: 16 (over z_lo, y, core), pair: 4 (over x).
Axes of the slice: x: 4, y: 4, z: 8 (z_hi: 4, z_lo: 2; z = z_hi * 2 + z_lo), core: 2. Of those that a mesh axis runs over, the one named last changes fastest.
Arguments:
- query_tokens: bfloat16 [4, 4, 32, 12, 32, 1536], P('pair', 'tm', 'height'), may hold values from -6.5 to 6.5
- key_tokens: bfloat16 [4, 4, 32, 12, 32, 1536], P('pair', 'tm', 'height'), may hold values from -6.5 to 6.5
- value_tokens: bfloat16 [4, 4, 32, 12, 32, 1536], P('pair', 'tm', 'height'), may hold values from -6 to 6
- head_weight: bfloat16 [1536, 64], replicated, may hold values from -0.15625 to 0.15625
- target_noise: bfloat16 [4, 4, 32, 12, 32, 64], P('pair', 'tm', 'height'), may hold values from -13 to 13
- far_owner: int32 [4, 4, 32, 12, 1], P('pair', 'tm', 'height'), may hold values from 0 to 15; in each aligned block of 24 rows (0 to 23, 24 to 47, ..., all dimensions but the last counted through in order) at most 2 rows name the same one
- far_offset: int32 [4, 4, 32, 12, 1], P('pair', 'tm', 'height'), may hold values from 0 to 23
- timestep: int32 [2], replicated, may hold values from 0 to 999
- labels: int32 [2], replicated, may hold values from 0 to 100
Outputs:
- weighted_error: bfloat16 [4, 4, 32, 12, 32, 64], P('pair', 'tm', 'height')
- clip_loss: float32 [4], P('pair')
- pair_margin: float32 [4], P('pair')
The draws below stay inside these ranges and needn't reach their ends.
Inputs may be any that keep to these rules, and one draw needn't show every extreme that they name: `far_owner`: among the 24 query tiles of one index of height (aligned blocks of rows), at most 2 references name one owner; the far tiles of one query tile have different owners.
All inputs are finite; a program needn't handle non-finite values.
Results may differ from the reference program's by a relative error of at most 0.0027.
Values may be sent and summed in bfloat16 or wider, within the bound.
No kernel may reach another device: no remote copies, remote signals or barrier semaphores. Data moves between devices by JAX's collectives and lax.ppermute only.
A program may use at most 256 MiB of HBM per device.

```python
import math
import jax
import jax.numpy as jnp
import numpy as np
from jax import lax

HEADS = 12
HD = 128
INNER = 1536
PATCH = 64
TILE = 32
CT = 12
RT_DEV = 2
K_FAR = 1
RATERS = 100
FT = 4
RT = 32
CLIPS = 4
PAIRS = 2
TILES_DEV = 24
CAP = 2
N_HEIGHT = 16


def draw_query_tokens(key, part):
    full_shape = (CLIPS, FT, RT, CT, TILE, INNER)
    key = jax.random.fold_in(key, 1)
    return jnp.clip(1.5 * jax.random.normal(key, full_shape, jnp.float32), -6.5, 6.5).astype(jnp.bfloat16)


def draw_key_tokens(key, part):
    full_shape = (CLIPS, FT, RT, CT, TILE, INNER)
    key = jax.random.fold_in(key, 2)
    return jnp.clip(1.5 * jax.random.normal(key, full_shape, jnp.float32), -6.5, 6.5).astype(jnp.bfloat16)


def draw_target_noise(key, part):
    key = jax.random.fold_in(key, 3)
    full_shape = (CLIPS, FT, RT, CT, TILE, PATCH)
    frames = lax.broadcasted_iota(jnp.int32, full_shape, 1).astype(jnp.float32)
    rows = lax.broadcasted_iota(jnp.int32, full_shape, 2).astype(jnp.float32)
    position = (frames * RT + rows) / (FT * RT - 1)
    noise = 0.4 * jnp.clip(jax.random.normal(key, full_shape, jnp.float32), -4.0, 4.0)
    clip_scale = jnp.exp(jax.random.uniform(jax.random.fold_in(key, 1), (CLIPS, 1, 1, 1, 1, 1), jnp.float32, -1.0, 1.0))
    rising = 1.0 + 2.0 * position
    return (noise * rising * clip_scale).astype(jnp.bfloat16)


def plant(values, key, least, largest):
    spot = [jax.random.randint(jax.random.fold_in(key, axis), (), 0, length) for axis, length in enumerate(values.shape)]
    widest = values.shape.index(max(values.shape))
    beside = spot[:widest] + [(spot[widest] + 1) % values.shape[widest]] + spot[widest + 1:]
    return values.at[tuple(spot)].set(least).at[tuple(beside)].set(largest)


def block_levels(rng, extent, shards, low, top_value):
    loudness, own = 1.0, jax.random.fold_in(rng, 6)
    for dim, shards_of in shards:
        draws = jnp.exp(jax.random.uniform(jax.random.fold_in(own, dim), (shards_of,), jnp.float32, low / len(shards), top_value / len(shards)))
        loudness = loudness * jnp.repeat(draws, extent[dim] // shards_of).reshape([-1 if axis == dim else 1 for axis in range(len(extent))])
    return loudness


def shared_out(rng, own, number, rows, count, top, bound, lean):
    sequence = jax.random.permutation(rng, count)
    crowded, ordinary = shares(count, rows * top, bound, lean, True), shares(count, rows * top, bound, lean, False)
    places = jnp.arange(count)

    def named(tallies, offset_by):
        used = int((tallies > 0).sum())
        fixed = max(1, used // 4)
        passed = fixed + (places - fixed + offset_by * (used - fixed)) % max(1, count - fixed)
        return jnp.zeros((count,), jnp.int32).at[sequence[jnp.where(places < fixed, places, passed)]].set(jnp.asarray(tallies, jnp.int32))

    tallies = jnp.where(number % 4 == 0, named(crowded, number // 4), named(ordinary, number - number // 4 - 1))
    mixed = jax.random.permutation(jax.random.fold_in(own, 3), count)
    source_of, receiver = mixed[0:count // 2 * 2:2], mixed[1:count // 2 * 2:2]
    margin = jnp.minimum(tallies[source_of] - 1, bound - tallies[receiver]) // 2
    margin = jnp.where((source_of == sequence[0]) | (receiver == sequence[0]) | (tallies[receiver] == 0), 0, jnp.maximum(margin, 0))
    passed = jax.random.randint(jax.random.fold_in(own, 4), (count // 2,), 0, 1 << 20) % (margin + 1)
    tallies = tallies.at[source_of].add(-passed).at[receiver].add(passed)
    items = jnp.searchsorted(jnp.cumsum(tallies), jnp.arange(rows * top), side="right").astype(jnp.int32)
    listing = items.reshape(top, rows).T
    listing = listing[jax.random.permutation(jax.random.fold_in(own, 1), rows)]
    offset_by = jax.random.randint(jax.random.fold_in(own, 2), (rows, 1), 0, top)
    return jnp.take_along_axis(listing, (jnp.arange(top)[None, :] + offset_by) % top, axis=1)


def shares(count, total, reach, skew, full):
    weights = [(1 << 20) // math.isqrt(rank ** skew) + 1 for rank in range(1, count + 1)]
    largest = reach if full else min(reach, max(-(-total // count), total * weights[0] // sum(weights)))
    least = 1 if total - largest >= count - 1 else 0
    holding, spare = [largest] + [least] * (count - 1), total - largest - least * (count - 1)
    while spare > 0:
        free = [i for i in range(1, count) if holding[i] < largest] or [i for i in range(1, count) if holding[i] < reach]
        whole, budget = sum([weights[i] for i in free]), spare
        for i in free:
            extra = min(reach - holding[i], max(1, budget * weights[i] // whole), spare)
            holding[i] = holding[i] + extra
            spare = spare - extra
    return np.array(holding)


def scatter_about(key, shape, scale, bound, pieces=(), kind=jnp.bfloat16):
    level = block_levels(key, shape, pieces, -0.22, 0.18) if pieces else 1.0
    drawn = jax.random.normal(key, shape, jnp.float32) * scale * level
    return jnp.minimum(jnp.maximum(drawn, -bound), bound).astype(kind)


def setup_inputs(seed: int = 0) -> dict:
    key_of = jax.random.split(jax.random.key(seed), 10)
    query_tokens = draw_query_tokens(jax.random.fold_in(key_of[9], 71), 0)
    key_tokens = draw_key_tokens(jax.random.fold_in(key_of[9], 71), 0)
    value_tokens = scatter_about(key_of[2], (CLIPS, FT, RT, CT, TILE, INNER), 1.0, 6.0, ((0, 4), (1, 4), (2, 16)))
    head_weight = scatter_about(key_of[3], (INNER, PATCH), INNER ** -0.5, 0.15625)
    target_noise = draw_target_noise(jax.random.fold_in(key_of[9], 71), 0)
    far_owner_keys = jax.random.split(jax.random.fold_in(key_of[5], 1), CLIPS * FT * RT * CT // TILES_DEV)
    far_owner_turns = jax.random.permutation(jax.random.fold_in(key_of[5], 3), CLIPS * FT * RT * CT // TILES_DEV)
    far_owner = jax.vmap(lambda own, number: shared_out(jax.random.fold_in(key_of[5], 2), own, number, TILES_DEV, N_HEIGHT, K_FAR, CAP, 2))(far_owner_keys, far_owner_turns).reshape((CLIPS, FT, RT, CT, K_FAR))
    far_offset = plant(jax.random.randint(key_of[6], (CLIPS, FT, RT, CT, K_FAR), 0, TILES_DEV), jax.random.fold_in(key_of[6], 1), 0, TILES_DEV - 1).astype(jnp.int32)
    timestep = jax.random.randint(key_of[7], (PAIRS,), 0, 1000).astype(jnp.int32)
    labels = jax.random.randint(key_of[8], (PAIRS,), 0, RATERS + 1).astype(jnp.int32)
    return {"query_tokens": query_tokens, "key_tokens": key_tokens, "value_tokens": value_tokens, "head_weight": head_weight, "target_noise": target_noise, "far_owner": far_owner, "far_offset": far_offset, "timestep": timestep, "labels": labels}


def attend_tile(query_tile, key_rows, token_ok):
    query_heads = query_tile.astype(jnp.float32).reshape(TILE, HEADS, HD)
    key_heads = key_rows[:, :INNER].astype(jnp.float32).reshape(-1, HEADS, HD)
    value_heads = key_rows[:, INNER:].astype(jnp.float32).reshape(-1, HEADS, HD)
    scores = jnp.einsum('qhd,khd->hqk', query_heads, key_heads) * (1.0 / math.sqrt(HD))
    scores = jnp.where(token_ok[None, None, :], scores, -1e+30)
    top_score = lax.optimization_barrier(jnp.max(scores, axis=2, keepdims=True))
    weights = jnp.exp(scores - top_score)
    total = lax.optimization_barrier(jnp.sum(weights, axis=2))
    rounded = lax.optimization_barrier(weights.astype(jnp.bfloat16)).astype(jnp.float32)
    mixed = jnp.einsum('hqk,khd->qhd', rounded, value_heads) / jnp.transpose(total)[:, :, None]
    return mixed.reshape(TILE, INNER).astype(jnp.bfloat16)

def reference(query_tokens, key_tokens, value_tokens, head_weight, target_noise, far_owner, far_offset, timestep, labels):
    keyval = jnp.concatenate([key_tokens, value_tokens], axis=5)
    padded = jnp.pad(keyval, ((0, 0), (1, 1), (1, 1), (1, 1), (0, 0), (0, 0)))
    inside = jnp.pad(jnp.ones((FT, RT, CT), jnp.float32), 1) > 0.5
    far_row = (far_owner * RT_DEV + far_offset // CT).astype(jnp.int32)
    far_col = (far_offset % CT).astype(jnp.int32)

    def tile_row(flat):
        clip_id = flat // (FT * RT)
        frame_id = flat // RT % FT
        row_id = flat % RT
        anchor = jnp.zeros((), jnp.int32)
        window = lax.dynamic_slice(padded, (clip_id, frame_id, row_id, anchor, anchor, anchor), (1, 3, 3, CT + 2, TILE, 2 * INNER))[0]
        window_ok = lax.dynamic_slice(inside, (frame_id, row_id, anchor), (3, 3, CT + 2))
        results = []
        for column in range(CT):
            near_rows = window[:, :, column:column + 3].reshape(27 * TILE, 2 * INNER)
            near_ok = window_ok[:, :, column:column + 3].reshape(27)
            far_list = [keyval[clip_id, frame_id, far_row[clip_id, frame_id, row_id, column, choose], far_col[clip_id, frame_id, row_id, column, choose]] for choose in range(K_FAR)]
            key_rows = jnp.concatenate([near_rows] + far_list, axis=0)
            tile_ok = jnp.concatenate([near_ok, jnp.ones((K_FAR,), jnp.bool_)])
            token_ok = jnp.repeat(tile_ok, TILE)
            results.append(attend_tile(query_tokens[clip_id, frame_id, row_id, column], key_rows, token_ok))
        return jnp.stack(results)
    attended = lax.map(tile_row, jnp.arange(CLIPS * FT * RT, dtype=jnp.int32))
    prediction = jnp.dot(attended.reshape(-1, INNER), head_weight, preferred_element_type=jnp.float32).reshape(CLIPS, -1)
    error = prediction - target_noise.astype(jnp.float32).reshape(CLIPS, -1)
    step_weight = 0.5 + (timestep.astype(jnp.float32) + 1.0) / 1000.0
    clip_weight = jnp.repeat(step_weight, 2)
    weighted_error = (jnp.sqrt(clip_weight)[:, None] * error).astype(jnp.bfloat16).reshape(target_noise.shape)
    clip_loss = clip_weight * lax.optimization_barrier(jnp.sum(error * error, axis=1)) / (FT * RT * CT * TILE * PATCH)
    paired = clip_loss.reshape(PAIRS, 2)
    strength = 2.0 * labels.astype(jnp.float32) / RATERS - 1.0
    pair_margin = jnp.repeat(strength * (paired[:, 1] - paired[:, 0]), 2)
    return (weighted_error, clip_loss, pair_margin)
```

```python
import functools
import math

import jax
import jax.numpy as jnp
from jax import lax
from jax.experimental import pallas as pl
from jax.experimental.pallas import tpu as pltpu
from jax.sharding import PartitionSpec as P

HEADS = 12
HD = 128
PATCH = 64
TILE = 32
RATERS = 100
SLOTS = 2
NEG = -1e30
FACTOR = math.log2(math.e) / math.sqrt(HD)
LSE_ROWS = 16
MIB = 1 << 20

NT = (((1,), (1,)), ((), ()))
NN = (((1,), (0,)), ((), ()))


def dot(a, b, dims):
    return lax.dot_general(a, b, dims, preferred_element_type=jnp.float32)


def lane_iota(shape):
    return lax.broadcasted_iota(jnp.int32, shape, 1)


def window_kernel(groups, columns, edge_ref, *refs):
    q_refs = refs[:groups]
    k_refs = refs[groups : groups + 3]
    v_refs = refs[groups + 3 : groups + 6]
    wt_ref = refs[groups + 6]
    p_refs = refs[groups + 7 : 2 * groups + 7]
    l_refs = refs[2 * groups + 7 : 3 * groups + 7]
    acc_refs = refs[3 * groups + 7 :]
    step = pl.program_id(0)
    span = 4 * TILE
    rows = 2 * TILE * groups

    @pl.when(step == 0)
    def _():
        for acc in acc_refs:
            acc[...] = jnp.zeros_like(acc)

    key_tile = lane_iota((rows, span)) // TILE
    query_tile = (lax.broadcasted_iota(jnp.int32, (rows, span), 0) // TILE) % 2
    biases = {}
    pairs = columns // 2
    for pair in range(pairs):
        first = min(max(2 * pair - 1, 0), columns - 4)
        shift = 2 * pair - first
        if shift not in biases:
            near = jnp.abs(key_tile - query_tile - shift) <= 1
            base = jnp.where(near, 0.0, NEG)
            biases[shift] = (base + edge_ref[0], base, base + edge_ref[1])
    for half in range(2):
        lanes = slice(half * HD, half * HD + HD)
        head = 2 * step + half
        wt = wt_ref[:, lanes]
        for pair in range(pairs):
            first = min(max(2 * pair - 1, 0), columns - 4)
            bias = biases[2 * pair - first]
            tokens = slice(2 * TILE * pair, 2 * TILE * (pair + 1))
            keys = slice(TILE * first, TILE * (first + 4))
            queries = [q[tokens, lanes] for q in q_refs]
            query = queries[0] if groups == 1 else jnp.concatenate(queries, axis=0)
            scores = [dot(query, k_refs[i][keys, lanes], NT) + bias[i] for i in range(3)]
            top = jnp.max(jnp.maximum(jnp.maximum(scores[0], scores[1]), scores[2]), axis=1, keepdims=True)
            weights = [jnp.exp2((s - top) * FACTOR) for s in scores]
            total = jnp.sum(weights[0] + weights[1] + weights[2], axis=1, keepdims=True)
            mixed = sum(dot(weights[i].astype(jnp.bfloat16), v_refs[i][keys, lanes], NN) for i in range(3))
            mixed = (mixed * (1.0 / total)).astype(jnp.bfloat16)
            projected = dot(wt, mixed, NT)
            lse = top * FACTOR + jnp.log2(total)
            for g in range(groups):
                part = slice(2 * TILE * g, 2 * TILE * (g + 1))
                p_refs[g][PATCH * half : PATCH * (half + 1), tokens] = projected[:, part]
                acc = acc_refs[g]
                held = acc[tokens, :]
                acc[tokens, :] = jnp.where(lane_iota(held.shape) == head, lse[part], held)

    @pl.when(step == pl.num_programs(0) - 1)
    def _():
        for g in range(groups):
            l_refs[g][...] = jnp.transpose(acc_refs[g][...])[:LSE_ROWS, :]


def window_attention(edge, queries, query_block, keys, values, wt, columns):
    groups = len(queries)
    tokens = columns * TILE
    inner = wt.shape[1]
    steps = inner // (2 * HD)

    def block(row):
        return pl.BlockSpec((tokens, 2 * HD), lambda i, row=row: (row, i))

    specs = [pl.BlockSpec(memory_space=pltpu.SMEM)]
    specs += [block(query_block) for _ in queries]
    specs += [block(row) for _, row in keys] + [block(row) for _, row in values]
    specs += [pl.BlockSpec((PATCH, 2 * HD), lambda i: (0, i))]
    operands = [edge, *queries, *[a for a, _ in keys], *[a for a, _ in values], wt]
    heads = inner // HD
    flops = 2 * groups * tokens * heads * 12 * TILE * HD * 2
    out = pl.pallas_call(
        functools.partial(window_kernel, groups, columns),
        grid=(steps,),
        in_specs=specs,
        out_specs=[pl.BlockSpec((2 * PATCH, tokens), lambda i: (i, 0))] * groups
        + [pl.BlockSpec((LSE_ROWS, tokens), lambda i: (0, 0))] * groups,
        out_shape=[jax.ShapeDtypeStruct((heads * PATCH, tokens), jnp.float32)] * groups
        + [jax.ShapeDtypeStruct((LSE_ROWS, tokens), jnp.float32)] * groups,
        scratch_shapes=[pltpu.VMEM((tokens, 128), jnp.float32)] * groups,
        compiler_params=pltpu.CompilerParams(vmem_limit_bytes=32 * MIB),
        cost_estimate=pl.CostEstimate(flops=flops, bytes_accessed=8 * MIB, transcendentals=flops // 512),
    )(*operands)
    return out[:groups], out[groups:]


def far_kernel(per_step, heads, index_ref, query_ref, key_ref, value_ref, wbd_ref, out_ref):
    step = pl.program_id(0)
    upper = lax.broadcasted_iota(jnp.int32, (2 * TILE, 2 * HD), 0) // TILE
    right = lane_iota((2 * TILE, 2 * HD)) // HD
    own_half = upper == right
    lane = lane_iota((TILE, 128))
    for s in range(per_step):
        tile = index_ref[step * per_step + s]
        start = pl.multiple_of(tile * TILE, TILE)
        rows = slice(s * TILE, (s + 1) * TILE)
        scores = []
        for j in range(heads // 2):
            lanes = slice(2 * j * HD, 2 * (j + 1) * HD)
            query = query_ref[rows, lanes]
            stacked = jnp.concatenate([query, query], axis=0)
            stacked = jnp.where(own_half, stacked, jnp.zeros_like(stacked))
            scores.append(dot(stacked, key_ref[pl.ds(start, TILE), lanes], NT))
        scores = jnp.concatenate(scores, axis=0)
        top = jnp.max(scores, axis=1, keepdims=True)
        weights = jnp.exp2((scores - top) * FACTOR)
        total = jnp.sum(weights, axis=1, keepdims=True)
        rounded = weights.astype(jnp.bfloat16)
        inverse = 1.0 / total
        lse = top * FACTOR + jnp.log2(total)
        sums = jnp.zeros((TILE, 128), jnp.float32)
        for j in range(heads // 2):
            lanes = slice(2 * j * HD, 2 * (j + 1) * HD)
            pair = slice(2 * j * TILE, 2 * (j + 1) * TILE)
            mixed = dot(rounded[pair], value_ref[pl.ds(start, TILE), lanes], NN) * inverse[pair]
            mixed = jnp.concatenate([mixed[:TILE, :HD], mixed[TILE:, HD:]], axis=1).astype(jnp.bfloat16)
            lanes_out = slice(2 * j * PATCH, 2 * (j + 1) * PATCH)
            out_ref[rows, lanes_out] = dot(mixed, wbd_ref[:, lanes_out], NN).astype(jnp.bfloat16)
            for half in range(2):
                head = 2 * j + half
                sums = jnp.where(lane % LSE_ROWS == head, lse[head * TILE : (head + 1) * TILE], sums)
        high = sums.astype(jnp.bfloat16).astype(jnp.float32)
        middle = (sums - high).astype(jnp.bfloat16).astype(jnp.float32)
        low = sums - high - middle
        parts = jnp.where(lane < LSE_ROWS, high, jnp.where(lane < 2 * LSE_ROWS, middle, low))
        out_ref[rows, heads * PATCH :] = parts.astype(jnp.bfloat16)


def far_attention(index, received, key, value, wbd):
    count = index.shape[0]
    inner = key.shape[1]
    heads = inner // HD
    per_step = 4
    width = heads * PATCH + 128
    return pl.pallas_call(
        functools.partial(far_kernel, per_step, heads),
        grid_spec=pltpu.PrefetchScalarGridSpec(
            num_scalar_prefetch=1,
            grid=(count // per_step,),
            in_specs=[
                pl.BlockSpec((per_step * TILE, inner), lambda i, _: (i, 0)),
                pl.BlockSpec(key.shape, lambda i, _: (0, 0)),
                pl.BlockSpec(value.shape, lambda i, _: (0, 0)),
                pl.BlockSpec(wbd.shape, lambda i, _: (0, 0)),
            ],
            out_specs=pl.BlockSpec((per_step * TILE, width), lambda i, _: (i, 0)),
        ),
        out_shape=jax.ShapeDtypeStruct((count * TILE, width), jnp.bfloat16),
        compiler_params=pltpu.CompilerParams(vmem_limit_bytes=40 * MIB),
        cost_estimate=pl.CostEstimate(flops=1 << 33, bytes_accessed=9 * MIB, transcendentals=1 << 20),
    )(index, received, key, value, wbd)


def log_sum(*parts):
    top = functools.reduce(jnp.maximum, parts)
    return top + jnp.log2(sum(jnp.exp2(p - top) for p in parts))


def weighted_sum(weights, projected, heads):
    return sum(weights[h : h + 1, :] * projected[PATCH * h : PATCH * (h + 1), :] for h in range(heads))


def base_kernel(heads, p_ref, l_ref, far_ref, p_out, l_out):
    far = jnp.transpose(far_ref[...].astype(jnp.float32))
    at = heads * PATCH
    far_lse = far[at : at + LSE_ROWS] + far[at + LSE_ROWS : at + 2 * LSE_ROWS]
    far_lse = far_lse + far[at + 2 * LSE_ROWS : at + 3 * LSE_ROWS]
    own_lse = l_ref[...]
    both = log_sum(own_lse, far_lse)
    own_weight = jnp.exp2(own_lse - both)
    far_weight = jnp.exp2(far_lse - both)
    l_out[...] = both
    for h in range(heads):
        rows = slice(PATCH * h, PATCH * (h + 1))
        p_out[rows, :] = own_weight[h : h + 1, :] * p_ref[rows, :] + far_weight[h : h + 1, :] * far[rows, :]


def whole(kernel, out_shape, cost, *operands, smem=0):
    specs = [pl.BlockSpec(memory_space=pltpu.SMEM)] * smem
    specs += [pl.BlockSpec(memory_space=pltpu.VMEM)] * (len(operands) - smem)
    return pl.pallas_call(
        kernel,
        in_specs=specs,
        out_specs=jax.tree.map(lambda _: pl.BlockSpec(memory_space=pltpu.VMEM), out_shape),
        out_shape=out_shape,
        compiler_params=pltpu.CompilerParams(vmem_limit_bytes=32 * MIB),
        cost_estimate=pl.CostEstimate(flops=cost, bytes_accessed=2 * MIB, transcendentals=1 << 14),
    )(*operands)


def scale_kernel(heads, pu, lu, bu, ou, pd, ld, bd, od, up_out, down_out):
    for p, l, b, o, out in ((pu, lu, bu, ou, up_out), (pd, ld, bd, od, down_out)):
        lse = l[...]
        weights = jnp.exp2(lse - log_sum(lse, b[...], o[...]))
        out[:PATCH, :] = weighted_sum(weights, p, heads)
        out[PATCH:, :] = lse


def final_kernel(heads, chunks, scalars, *refs):
    target = refs[4 * chunks]
    error_out, sum_out = refs[4 * chunks + 1 :]
    total = jnp.zeros((1, 1), jnp.float32)
    for c in range(chunks):
        p, l, above, below = refs[4 * c : 4 * c + 4]
        lse = l[...]
        sums = log_sum(lse, above[PATCH:, :] + scalars[1], below[PATCH:, :] + scalars[2])
        out = weighted_sum(jnp.exp2(lse - sums), p, heads) + above[:PATCH, :] + below[:PATCH, :]
        prediction = jnp.transpose(out)
        tokens = prediction.shape[0]
        rows = slice(c * tokens, (c + 1) * tokens)
        error = prediction - target[rows, :].astype(jnp.float32)
        error_out[rows, :] = (scalars[0] * error).astype(jnp.bfloat16)
        total = total + jnp.sum(error * error, keepdims=True)
    sum_out[...] = jnp.broadcast_to(total, sum_out.shape)


def body(
    query_tokens,
    key_tokens,
    value_tokens,
    head_weight,
    target_noise,
    far_owner,
    far_offset,
    timestep,
    labels,
):
    _, _, rows_dev, columns, tile_len, inner = query_tokens.shape
    tiles = rows_dev * columns
    heads = inner // HD
    row_tokens = columns * tile_len
    tokens = rows_dev * row_tokens
    pairs_n, frames_n, height_n = (lax.axis_size(a) for a in ("pair", "tm", "height"))
    frame = lax.axis_index("tm")
    height = lax.axis_index("height")

    up_frames = [(i, i + 1) for i in range(frames_n - 1)]
    down_frames = [(i + 1, i) for i in range(frames_n - 1)]
    up_rows = [(i, i + 1) for i in range(height_n - 1)]
    down_rows = [(i + 1, i) for i in range(height_n - 1)]

    query = query_tokens.reshape(tokens, inner)
    key = key_tokens.reshape(tokens, inner)
    value = value_tokens.reshape(tokens, inner)

    last = jnp.concatenate([key[row_tokens:], value[row_tokens:]], axis=0)
    initial = jnp.concatenate([key[:row_tokens], value[:row_tokens]], axis=0)
    halo_before = lax.ppermute(last, "height", up_rows)
    halo_after = lax.ppermute(initial, "height", down_rows)

    owners = far_owner.reshape(tiles)
    offsets = far_offset.reshape(tiles)
    ids = jnp.arange(tiles)
    earlier = (ids[:, None] > ids[None, :]) & (owners[:, None] == owners[None, :])
    slot = owners * SLOTS + jnp.sum(earlier.astype(jnp.int32), axis=1)
    slot_count = height_n * SLOTS
    chosen = slot[:, None] == jnp.arange(slot_count)[None, :]
    source = jnp.sum(jnp.where(chosen, ids[:, None], 0), axis=0)
    marks = jnp.broadcast_to(offsets.astype(jnp.bfloat16)[:, None, None], (tiles, tile_len, 128))
    payload = jnp.concatenate([query.reshape(tiles, tile_len, inner), marks], axis=2)[source]
    received = lax.all_to_all(payload, "height", split_axis=0, concat_axis=0, tiled=True)

    from_below = []
    from_above = []
    for r in range(rows_dev):
        part = query[r * row_tokens : (r + 1) * row_tokens]
        from_below.append(lax.ppermute(part, "tm", up_frames))
        from_above.append(lax.ppermute(part, "tm", down_frames))

    wt = jnp.transpose(head_weight)
    paired = head_weight.reshape(heads // 2, 2, HD, PATCH)
    wbd = jnp.zeros((2, HD, heads // 2, 2, PATCH), head_weight.dtype)
    for half in range(2):
        wbd = wbd.at[half, :, :, half, :].set(jnp.transpose(paired[:, half], (1, 0, 2)))
    wbd = wbd.reshape(2 * HD, heads * PATCH)

    first_edge = jnp.where(height == 0, NEG, 0.0).astype(jnp.float32)
    last_edge = jnp.where(height == height_n - 1, NEG, 0.0).astype(jnp.float32)
    zero = jnp.zeros((), jnp.float32)

    def attend(r, queries, block):
        before = (halo_before, 0, halo_before, 1) if r == 0 else (key, r - 1, value, r - 1)
        after = (halo_after, 0, halo_after, 1) if r == rows_dev - 1 else (key, r + 1, value, r + 1)
        edge = jnp.stack([first_edge if r == 0 else zero, last_edge if r == rows_dev - 1 else zero])
        keys = [before[:2], (key, r), after[:2]]
        values = [before[2:], (value, r), after[2:]]
        return window_attention(edge, queries, block, keys, values, wt, columns)

    own = []
    for r in range(rows_dev):
        (p,), (l,) = attend(r, [query], r)
        own.append((p, l))

    index = received[:, 0, inner].astype(jnp.int32)
    returned = far_attention(index, received.reshape(slot_count * tile_len, inner + 128), key, value, wbd)
    width = returned.shape[1]
    returned = lax.all_to_all(
        returned.reshape(slot_count, tile_len, width), "height", split_axis=0, concat_axis=0, tiled=True
    )
    far = returned[slot].reshape(tokens, width)

    base = []
    for r in range(rows_dev):
        p, l = own[r]
        shapes = [jax.ShapeDtypeStruct(p.shape, p.dtype), jax.ShapeDtypeStruct(l.shape, l.dtype)]
        base.append(
            whole(
                functools.partial(base_kernel, heads),
                shapes,
                1 << 22,
                p,
                l,
                far[r * row_tokens : (r + 1) * row_tokens],
            )
        )
    base_lse = jnp.concatenate([l for _, l in base], axis=1)
    base_below = lax.ppermute(base_lse, "tm", up_frames)
    base_above = lax.ppermute(base_lse, "tm", down_frames)

    swap = [(i, i + 2) for i in range(frames_n - 2)] + [(i + 2, i) for i in range(frames_n - 2)]
    low = frame < frames_n - 2
    final_args = []
    for r in range(rows_dev):
        cols = slice(r * row_tokens, (r + 1) * row_tokens)
        (pd, pu), (ld, lu) = attend(r, [from_below[r], from_above[r]], 0)
        other = lax.ppermute(jnp.where(low, lu, ld), "tm", swap)
        other_u = jnp.where(low, other, NEG)
        other_d = jnp.where(low, NEG, other)
        shape = jax.ShapeDtypeStruct((PATCH + LSE_ROWS, row_tokens), jnp.float32)
        to_above, to_below = whole(
            functools.partial(scale_kernel, heads),
            [shape, shape],
            1 << 22,
            pu,
            lu,
            base_above[:, cols],
            other_u,
            pd,
            ld,
            base_below[:, cols],
            other_d,
        )
        got_below = lax.ppermute(to_above, "tm", up_frames)
        got_above = lax.ppermute(to_below, "tm", down_frames)
        final_args += [*base[r], got_above, got_below]

    pair = lax.axis_index("pair")
    pair_slot = pair // 2
    step_weight = 0.5 + (timestep[pair_slot].astype(jnp.float32) + 1.0) / 1000.0
    no_above = jnp.where(frame == frames_n - 1, NEG, 0.0).astype(jnp.float32)
    no_below = jnp.where(frame == 0, NEG, 0.0).astype(jnp.float32)
    scalars = jnp.stack([jnp.sqrt(step_weight), no_above, no_below])
    error, squares = whole(
        functools.partial(final_kernel, heads, rows_dev),
        [jax.ShapeDtypeStruct((tokens, PATCH), jnp.bfloat16), jax.ShapeDtypeStruct((8, 128), jnp.float32)],
        1 << 22,
        scalars,
        *final_args,
        target_noise.reshape(tokens, PATCH),
        smem=1,
    )
    weighted_error = error.reshape(target_noise.shape)

    devices = pairs_n * frames_n * height_n
    spread = jnp.broadcast_to(squares[:1], (devices, 128))
    gathered = lax.all_to_all(spread, ("pair", "tm", "height"), split_axis=0, concat_axis=0, tiled=True)
    sums = jnp.sum(gathered.reshape(pairs_n, frames_n * height_n, 128)[:, :, 0], axis=1)
    count = frames_n * height_n * tokens * PATCH
    mine = sums[pair]
    partner = sums[pair ^ 1]
    clip_loss = step_weight * mine / count
    partner_loss = step_weight * partner / count
    difference = jnp.where(pair % 2 == 1, clip_loss - partner_loss, partner_loss - clip_loss)
    strength = 2.0 * labels[pair_slot].astype(jnp.float32) / RATERS - 1.0
    return (weighted_error, clip_loss.reshape(1), (strength * difference).reshape(1))


def solution(mesh):
    placed = (
        P("pair", "tm", "height", None, None, None),
        P("pair", "tm", "height", None, None, None),
        P("pair", "tm", "height", None, None, None),
        P(),
        P("pair", "tm", "height", None, None, None),
        P("pair", "tm", "height", None, None),
        P("pair", "tm", "height", None, None),
        P(),
        P(),
    )
    return jax.shard_map(
        body,
        mesh=mesh,
        in_specs=placed,
        out_specs=(P("pair", "tm", "height", None, None, None), P("pair"), P("pair")),
        check_vma=False,
    )
```

```python
import functools
import math

import jax
import jax.numpy as jnp
from jax import lax
from jax.experimental import pallas as pl
from jax.experimental.pallas import tpu as pltpu
from jax.sharding import PartitionSpec as P

HEADS = 12
HD = 128
PATCH = 64
TILE = 32
RATERS = 100
SLOTS = 2
NEG = -1e30
FACTOR = math.log2(math.e) / math.sqrt(HD)
LSE_ROWS = 16
MIB = 1 << 20

NT = (((1,), (1,)), ((), ()))
NN = (((1,), (0,)), ((), ()))


def dot(a, b, dims):
    return lax.dot_general(a, b, dims, preferred_element_type=jnp.float32)


def lane_iota(shape):
    return lax.broadcasted_iota(jnp.int32, shape, 1)


def window_kernel(groups, columns, edge_ref, *refs):
    q_refs = refs[:groups]
    k_refs = refs[groups : groups + 3]
    v_refs = refs[groups + 3 : groups + 6]
    wt_ref = refs[groups + 6]
    p_refs = refs[-3 * groups : -2 * groups]
    l_refs = refs[-2 * groups : -groups]
    acc_refs = refs[-groups:]
    step = pl.program_id(0)
    span = 4 * TILE
    rows = 2 * TILE * groups

    @pl.when(step == 0)
    def _():
        for acc in acc_refs:
            acc[...] = jnp.zeros_like(acc)

    key_tile = lane_iota((rows, span)) // TILE
    query_tile = (lax.broadcasted_iota(jnp.int32, (rows, span), 0) // TILE) % 2
    biases = {}
    pairs = columns // 2
    for pair in range(pairs):
        first = min(max(2 * pair - 1, 0), columns - 4)
        shift = 2 * pair - first
        if shift not in biases:
            near = jnp.abs(key_tile - query_tile - shift) <= 1
            base = jnp.where(near, 0.0, NEG)
            biases[shift] = (base + edge_ref[0], base, base + edge_ref[1])
    for half in range(2):
        lanes = slice(half * HD, half * HD + HD)
        wt = wt_ref[:, lanes]
        scores = []
        for pair in range(pairs):
            first = min(max(2 * pair - 1, 0), columns - 4)
            bias = biases[2 * pair - first]
            tokens = slice(2 * TILE * pair, 2 * TILE * (pair + 1))
            keys = slice(TILE * first, TILE * (first + 4))
            queries = [q[tokens, lanes] for q in q_refs]
            query = queries[0] if groups == 1 else jnp.concatenate(queries, axis=0)
            raw = dot(query, jnp.concatenate([k[keys, lanes] for k in k_refs], axis=0), NT)
            scores.append([raw[:, span * i : span * (i + 1)] + bias[i] for i in range(3)])
        tops = [jnp.max(functools.reduce(jnp.maximum, s), axis=1, keepdims=True) for s in scores]
        weights = [[jnp.exp2((x - top) * FACTOR) for x in s] for s, top in zip(scores, tops)]
        totals = [jnp.sum(sum(w), axis=1, keepdims=True) for w in weights]
        mixed = []
        for pair, weight in enumerate(weights):
            first = min(max(2 * pair - 1, 0), columns - 4)
            keys = slice(TILE * first, TILE * (first + 4))
            rounded = jnp.concatenate([w.astype(jnp.bfloat16) for w in weight], axis=1)
            mixed.append(dot(rounded, jnp.concatenate([v[keys, lanes] for v in v_refs], axis=0), NN))
        mixed = [(m * (1.0 / total)).astype(jnp.bfloat16) for m, total in zip(mixed, totals)]
        projected = [dot(wt, m, NT) for m in mixed]
        for pair in range(pairs):
            tokens = slice(2 * TILE * pair, 2 * TILE * (pair + 1))
            lse = tops[pair] * FACTOR + jnp.log2(totals[pair])
            for g in range(groups):
                part = slice(2 * TILE * g, 2 * TILE * (g + 1))
                p_refs[g][PATCH * half : PATCH * (half + 1), tokens] = projected[pair][:, part]
                held = acc_refs[g][tokens, :]
                mark = lane_iota(held.shape) == 2 * step + half
                acc_refs[g][tokens, :] = jnp.where(mark, lse[part], held)

    @pl.when(step == pl.num_programs(0) - 1)
    def _():
        for g in range(groups):
            l_refs[g][...] = jnp.transpose(acc_refs[g][...])[:LSE_ROWS, :]


def window_attention(edge, queries, query_block, keys, values, wt, columns, after=()):
    groups = len(queries)
    tokens = columns * TILE
    inner = wt.shape[1]
    steps = inner // (2 * HD)

    def block(row):
        return pl.BlockSpec((tokens, 2 * HD), lambda i, row=row: (row, i))

    specs = [pl.BlockSpec(memory_space=pltpu.SMEM)]
    specs += [block(query_block) for _ in queries]
    specs += [block(row) for _, row in keys] + [block(row) for _, row in values]
    specs += [pl.BlockSpec((PATCH, 2 * HD), lambda i: (0, i))]
    specs += [pl.BlockSpec(memory_space=pl.ANY)] * len(after)
    operands = [edge, *queries, *[a for a, _ in keys], *[a for a, _ in values], wt, *after]
    heads = inner // HD
    flops = 2 * groups * tokens * heads * 12 * TILE * HD * 2
    out = pl.pallas_call(
        functools.partial(window_kernel, groups, columns),
        grid=(steps,),
        in_specs=specs,
        out_specs=[pl.BlockSpec((2 * PATCH, tokens), lambda i: (i, 0))] * groups
        + [pl.BlockSpec((LSE_ROWS, tokens), lambda i: (0, 0))] * groups,
        out_shape=[jax.ShapeDtypeStruct((heads * PATCH, tokens), jnp.float32)] * groups
        + [jax.ShapeDtypeStruct((LSE_ROWS, tokens), jnp.float32)] * groups,
        scratch_shapes=[pltpu.VMEM((tokens, 128), jnp.float32)] * groups,
        compiler_params=pltpu.CompilerParams(vmem_limit_bytes=56 * MIB),
        cost_estimate=pl.CostEstimate(flops=1, bytes_accessed=1, transcendentals=0),
    )(*operands)
    return out[:groups], out[groups:]


def far_kernel(per_step, heads, index_ref, query_ref, key_ref, value_ref, wbd_ref, out_ref, lse_ref):
    step = pl.program_id(0)
    upper = lax.broadcasted_iota(jnp.int32, (2 * TILE, 2 * HD), 0) // TILE
    right = lane_iota((2 * TILE, 2 * HD)) // HD
    own_half = upper == right
    lane = lane_iota((TILE, 128))
    slots = range(per_step)
    pairs = range(heads // 2)
    starts = [pl.multiple_of(index_ref[step * per_step + s] * TILE, TILE) for s in slots]
    scores = []
    for s in slots:
        parts = []
        for j in pairs:
            lanes = slice(2 * j * HD, 2 * (j + 1) * HD)
            query = query_ref[s * TILE : (s + 1) * TILE, lanes]
            stacked = jnp.concatenate([query, query], axis=0)
            stacked = jnp.where(own_half, stacked, jnp.zeros_like(stacked))
            parts.append(dot(stacked, key_ref[pl.ds(starts[s], TILE), lanes], NT))
        scores.append(jnp.concatenate(parts, axis=0))
    tops = [jnp.max(x, axis=1, keepdims=True) for x in scores]
    weights = [jnp.exp2((x - top) * FACTOR) for x, top in zip(scores, tops)]
    totals = [jnp.sum(w, axis=1, keepdims=True) for w in weights]
    rounded = [w.astype(jnp.bfloat16) for w in weights]
    inverse = [1.0 / total for total in totals]
    lses = [top * FACTOR + jnp.log2(total) for top, total in zip(tops, totals)]
    mixed = []
    for s in slots:
        for j in pairs:
            lanes = slice(2 * j * HD, 2 * (j + 1) * HD)
            pair = slice(2 * j * TILE, 2 * (j + 1) * TILE)
            both = dot(rounded[s][pair], value_ref[pl.ds(starts[s], TILE), lanes], NN) * inverse[s][pair]
            mixed.append(jnp.concatenate([both[:TILE, :HD], both[TILE:, HD:]], axis=1).astype(jnp.bfloat16))
    for j in pairs:
        lanes = slice(2 * j * PATCH, 2 * (j + 1) * PATCH)
        stacked = jnp.concatenate([mixed[s * (heads // 2) + j] for s in slots], axis=0)
        out_ref[:, lanes] = dot(stacked, wbd_ref[:, lanes], NN).astype(jnp.bfloat16)
    sums = []
    for s in slots:
        column = jnp.zeros((TILE, 128), jnp.float32)
        for head in range(heads):
            column = jnp.where(lane == head, lses[s][head * TILE : (head + 1) * TILE], column)
        sums.append(column)
    turned = jnp.transpose(jnp.concatenate(sums, axis=0))[:LSE_ROWS]
    for o in range(per_step // SLOTS):
        lse_ref[o] = turned[:, o * SLOTS * TILE : (o + 1) * SLOTS * TILE]


def far_attention(index, received, key, value, wbd):
    count = index.shape[0]
    inner = key.shape[1]
    heads = inner // HD
    per_step = 4
    width = heads * PATCH
    return pl.pallas_call(
        functools.partial(far_kernel, per_step, heads),
        grid_spec=pltpu.PrefetchScalarGridSpec(
            num_scalar_prefetch=1,
            grid=(count // per_step,),
            in_specs=[
                pl.BlockSpec((per_step * TILE, inner), lambda i, _: (i, 0)),
                pl.BlockSpec(key.shape, lambda i, _: (0, 0)),
                pl.BlockSpec(value.shape, lambda i, _: (0, 0)),
                pl.BlockSpec(wbd.shape, lambda i, _: (0, 0)),
            ],
            out_specs=[
                pl.BlockSpec((per_step * TILE, width), lambda i, _: (i, 0)),
                pl.BlockSpec((per_step // SLOTS, LSE_ROWS, SLOTS * TILE), lambda i, _: (i, 0, 0)),
            ],
        ),
        out_shape=[
            jax.ShapeDtypeStruct((count * TILE, width), jnp.bfloat16),
            jax.ShapeDtypeStruct((count // SLOTS, LSE_ROWS, SLOTS * TILE), jnp.float32),
        ],
        compiler_params=pltpu.CompilerParams(vmem_limit_bytes=56 * MIB),
        cost_estimate=pl.CostEstimate(flops=1, bytes_accessed=1, transcendentals=0),
    )(index, received, key, value, wbd)


def log_sum(*parts):
    top = functools.reduce(jnp.maximum, parts)
    return top + jnp.log2(sum(jnp.exp2(p - top) for p in parts))


def weighted_sum(weights, projected, heads):
    return sum(weights[h : h + 1, :] * projected[PATCH * h : PATCH * (h + 1), :] for h in range(heads))


def base_kernel(row_tiles, slot_ref, far_ref, *refs):
    own_refs = refs[:-2]
    far_out, base_out = refs[-2:]
    for r, own_ref in enumerate(own_refs):
        for c in range(row_tiles):
            slot = slot_ref[r * row_tiles + c]
            held = far_ref[slot // SLOTS]
            far = jnp.where(slot % SLOTS == 0, held[:, :TILE], held[:, TILE:])
            lanes = slice((r * row_tiles + c) * TILE, (r * row_tiles + c + 1) * TILE)
            far_out[:, lanes] = far
            base_out[:, lanes] = log_sum(own_ref[:, c * TILE : (c + 1) * TILE], far)


def tie(value, after):
    def kernel(*refs):
        pass

    anywhere = pl.BlockSpec(memory_space=pl.ANY)
    return pl.pallas_call(
        kernel,
        in_specs=[anywhere] * (1 + len(after)),
        out_specs=anywhere,
        out_shape=jax.ShapeDtypeStruct(value.shape, value.dtype),
        input_output_aliases={0: 0},
    )(value, *after)


def merge_kernel(heads, chunks, base, far_l, far_p, *refs):
    out = refs[-1]
    for c in range(chunks):
        p, l = refs[2 * c : 2 * c + 2]
        tokens = l.shape[1]
        cols = slice(c * tokens, (c + 1) * tokens)
        far = jnp.transpose(far_p[cols, :].astype(jnp.float32))
        own_weight = jnp.exp2(l[...] - base[:, cols])
        far_weight = jnp.exp2(far_l[:, cols] - base[:, cols])
        for h in range(heads):
            rows = slice(PATCH * h, PATCH * (h + 1))
            out[rows, cols] = own_weight[h : h + 1, :] * p[rows, :] + far_weight[h : h + 1, :] * far[rows, :]


def whole(kernel, out_shape, cost, *operands, smem=0):
    specs = [pl.BlockSpec(memory_space=pltpu.SMEM)] * smem
    specs += [pl.BlockSpec(memory_space=pltpu.VMEM)] * (len(operands) - smem)
    return pl.pallas_call(
        kernel,
        in_specs=specs,
        out_specs=jax.tree.map(lambda _: pl.BlockSpec(memory_space=pltpu.VMEM), out_shape),
        out_shape=out_shape,
        compiler_params=pltpu.CompilerParams(vmem_limit_bytes=56 * MIB),
        cost_estimate=pl.CostEstimate(flops=1, bytes_accessed=1, transcendentals=0),
    )(*operands)


def scale_kernel(heads, chunks, flags, other, *refs):
    up_out, down_out = refs[-2:]
    for side, out in enumerate((up_out, down_out)):
        base = refs[2 * chunks * 2 + side]
        for c in range(chunks):
            p, l = refs[2 * (chunks * side + c) : 2 * (chunks * side + c) + 2]
            tokens = l.shape[1]
            cols = slice(c * tokens, (c + 1) * tokens)
            lse = l[...]
            weights = jnp.exp2(lse - log_sum(lse, base[:, cols], other[:, cols] + flags[side]))
            out[:PATCH, cols] = weighted_sum(weights, p, heads)
            out[PATCH:, cols] = lse


def final_kernel(heads, scalars, p, l, above, below, target, error_out, sum_out):
    lse = l[...]
    sums = log_sum(lse, above[PATCH:, :] + scalars[1], below[PATCH:, :] + scalars[2])
    out = weighted_sum(jnp.exp2(lse - sums), p, heads) + above[:PATCH, :] + below[:PATCH, :]
    error = jnp.transpose(out) - target[...].astype(jnp.float32)
    error_out[...] = (scalars[0] * error).astype(jnp.bfloat16)
    sum_out[...] = jnp.broadcast_to(jnp.sum(error * error, keepdims=True), sum_out.shape)


def body(
    query_tokens,
    key_tokens,
    value_tokens,
    head_weight,
    target_noise,
    far_owner,
    far_offset,
    timestep,
    labels,
):
    _, _, rows_dev, columns, tile_len, inner = query_tokens.shape
    tiles = rows_dev * columns
    heads = inner // HD
    row_tokens = columns * tile_len
    tokens = rows_dev * row_tokens
    pairs_n, frames_n, height_n = (lax.axis_size(a) for a in ("pair", "tm", "height"))
    frame = lax.axis_index("tm")
    height = lax.axis_index("height")

    up_frames = [(i, i + 1) for i in range(frames_n - 1)]
    down_frames = [(i + 1, i) for i in range(frames_n - 1)]
    up_rows = [(i, i + 1) for i in range(height_n - 1)]
    down_rows = [(i + 1, i) for i in range(height_n - 1)]

    query = query_tokens.reshape(tokens, inner)
    key = key_tokens.reshape(tokens, inner)
    value = value_tokens.reshape(tokens, inner)

    last = jnp.concatenate([key[row_tokens:], value[row_tokens:]], axis=0)
    initial = jnp.concatenate([key[:row_tokens], value[:row_tokens]], axis=0)
    halo_before = lax.ppermute(last, "height", up_rows)
    halo_after = lax.ppermute(initial, "height", down_rows)

    owners = far_owner.reshape(tiles)
    offsets = far_offset.reshape(tiles)
    ids = jnp.arange(tiles)
    earlier = (ids[:, None] > ids[None, :]) & (owners[:, None] == owners[None, :])
    slot = owners * SLOTS + jnp.sum(earlier.astype(jnp.int32), axis=1)
    slot_count = height_n * SLOTS
    chosen = slot[:, None] == jnp.arange(slot_count)[None, :]
    source = jnp.sum(jnp.where(chosen, ids[:, None], 0), axis=0)
    marks = jnp.broadcast_to(offsets.astype(jnp.bfloat16)[:, None, None], (tiles, tile_len, 128))
    payload = jnp.concatenate([query.reshape(tiles, tile_len, inner), marks], axis=2)[source]
    received = lax.all_to_all(payload, "height", split_axis=0, concat_axis=0, tiled=True)

    from_below = lax.ppermute(query, "tm", up_frames)
    from_above = lax.ppermute(query, "tm", down_frames)

    wt = jnp.transpose(head_weight)
    paired = head_weight.reshape(heads // 2, 2, HD, PATCH)
    wbd = jnp.zeros((2, HD, heads // 2, 2, PATCH), head_weight.dtype)
    for half in range(2):
        wbd = wbd.at[half, :, :, half, :].set(jnp.transpose(paired[:, half], (1, 0, 2)))
    wbd = wbd.reshape(2 * HD, heads * PATCH)

    first_edge = jnp.where(height == 0, NEG, 0.0).astype(jnp.float32)
    last_edge = jnp.where(height == height_n - 1, NEG, 0.0).astype(jnp.float32)
    zero = jnp.zeros((), jnp.float32)

    def attend(r, queries, block, first=()):
        before = (halo_before, 0, halo_before, 1) if r == 0 else (key, r - 1, value, r - 1)
        after = (halo_after, 0, halo_after, 1) if r == rows_dev - 1 else (key, r + 1, value, r + 1)
        edge = jnp.stack([first_edge if r == 0 else zero, last_edge if r == rows_dev - 1 else zero])
        keys = [before[:2], (key, r), after[:2]]
        values = [before[2:], (value, r), after[2:]]
        return window_attention(edge, queries, block, keys, values, wt, columns, first)

    own, ups, downs = [], [], []
    for r in range(rows_dev):
        ps, ls = attend(r, [query, from_below, from_above], r)
        for held, p, l in zip((own, downs, ups), ps, ls):
            held.append((p, l))

    index = received[:, 0, inner].astype(jnp.int32)
    received = received.reshape(slot_count * tile_len, inner + 128)
    far_p, far_l = far_attention(index, received, key, value, wbd)
    far_l = lax.all_to_all(far_l, "height", split_axis=0, concat_axis=0, tiled=True)
    flat = jax.ShapeDtypeStruct((LSE_ROWS, tokens), jnp.float32)
    far_l, base_lse = whole(
        functools.partial(base_kernel, columns), [flat, flat], 0, slot, far_l, *[l for _, l in own], smem=1
    )
    base_below = lax.ppermute(base_lse, "tm", up_frames)
    base_above = lax.ppermute(base_lse, "tm", down_frames)

    swap = [(i, i + 2) for i in range(frames_n - 2)] + [(i + 2, i) for i in range(frames_n - 2)]
    low = frame < frames_n - 2
    width = far_p.shape[1]
    far_p = tie(far_p, [from_below, from_above])
    far_p = lax.all_to_all(
        far_p.reshape(slot_count, tile_len, width), "height", split_axis=0, concat_axis=0, tiled=True
    )
    base_p = whole(
        functools.partial(merge_kernel, heads, rows_dev),
        jax.ShapeDtypeStruct((width, tokens), jnp.float32),
        0,
        base_lse,
        far_l,
        far_p[slot].reshape(tokens, width),
        *[a for part in own for a in part],
    )
    lse_u = jnp.concatenate([l for _, l in ups], axis=1)
    lse_d = jnp.concatenate([l for _, l in downs], axis=1)
    other = lax.ppermute(jnp.where(low, lse_u, lse_d), "tm", swap)
    flags = jnp.where(low, jnp.array([0.0, NEG]), jnp.array([NEG, 0.0])).astype(jnp.float32)
    shape = jax.ShapeDtypeStruct((PATCH + LSE_ROWS, tokens), jnp.float32)
    to_above, to_below = whole(
        functools.partial(scale_kernel, heads, rows_dev),
        [shape, shape],
        0,
        flags,
        other,
        *[a for part in ups + downs for a in part],
        base_above,
        base_below,
        smem=1,
    )
    got_below = lax.ppermute(to_above, "tm", up_frames)
    got_above = lax.ppermute(to_below, "tm", down_frames)

    pair = lax.axis_index("pair")
    pair_slot = pair // 2
    step_weight = 0.5 + (timestep[pair_slot].astype(jnp.float32) + 1.0) / 1000.0
    no_above = jnp.where(frame == frames_n - 1, NEG, 0.0).astype(jnp.float32)
    no_below = jnp.where(frame == 0, NEG, 0.0).astype(jnp.float32)
    scalars = jnp.stack([jnp.sqrt(step_weight), no_above, no_below])
    error, squares = whole(
        functools.partial(final_kernel, heads),
        [jax.ShapeDtypeStruct((tokens, PATCH), jnp.bfloat16), jax.ShapeDtypeStruct((pairs_n * frames_n * height_n, 128), jnp.float32)],
        1 << 22,
        scalars,
        base_p,
        base_lse,
        got_above,
        got_below,
        target_noise.reshape(tokens, PATCH),
        smem=1,
    )
    weighted_error = error.reshape(target_noise.shape)

    gathered = lax.all_to_all(squares, ("pair", "tm", "height"), split_axis=0, concat_axis=0, tiled=True)
    sums = jnp.sum(gathered.reshape(pairs_n, frames_n * height_n, 128)[:, :, 0], axis=1)
    count = frames_n * height_n * tokens * PATCH
    mine = sums[pair]
    partner = sums[pair ^ 1]
    clip_loss = step_weight * mine / count
    partner_loss = step_weight * partner / count
    difference = jnp.where(pair % 2 == 1, clip_loss - partner_loss, partner_loss - clip_loss)
    strength = 2.0 * labels[pair_slot].astype(jnp.float32) / RATERS - 1.0
    return (weighted_error, clip_loss.reshape(1), (strength * difference).reshape(1))


def solution(mesh):
    placed = (
        P("pair", "tm", "height", None, None, None),
        P("pair", "tm", "height", None, None, None),
        P("pair", "tm", "height", None, None, None),
        P(),
        P("pair", "tm", "height", None, None, None),
        P("pair", "tm", "height", None, None),
        P("pair", "tm", "height", None, None),
        P(),
        P(),
    )
    return jax.shard_map(
        body,
        mesh=mesh,
        in_specs=placed,
        out_specs=(P("pair", "tm", "height", None, None, None), P("pair"), P("pair")),
        check_vma=False,
    )
```

```python
import functools
import math

import jax
import jax.numpy as jnp
from jax import lax
from jax.experimental import pallas as pl
from jax.experimental.pallas import tpu as pltpu
from jax.sharding import PartitionSpec as P

HEADS = 12
HD = 128
PATCH = 64
TILE = 32
RATERS = 100
SLOTS = 2
NEG = -1e30
FACTOR = math.log2(math.e) / math.sqrt(HD)
LSE_ROWS = 16
MIB = 1 << 20

NT = (((1,), (1,)), ((), ()))
NN = (((1,), (0,)), ((), ()))


def dot(a, b, dims):
    return lax.dot_general(a, b, dims, preferred_element_type=jnp.float32)


def lane_iota(shape):
    return lax.broadcasted_iota(jnp.int32, shape, 1)


def window_kernel(groups, columns, edge_ref, *refs):
    q_refs = refs[:groups]
    k_refs = refs[groups : groups + 3]
    v_refs = refs[groups + 3 : groups + 6]
    wt_ref = refs[groups + 6]
    p_refs = refs[-3 * groups : -2 * groups]
    l_refs = refs[-2 * groups : -groups]
    acc_refs = refs[-groups:]
    step = pl.program_id(0)
    span = 4 * TILE
    rows = 2 * TILE * groups

    @pl.when(step == 0)
    def _():
        for acc in acc_refs:
            acc[...] = jnp.zeros_like(acc)

    key_tile = lane_iota((rows, span)) // TILE
    query_tile = (lax.broadcasted_iota(jnp.int32, (rows, span), 0) // TILE) % 2
    biases = {}
    pairs = columns // 2
    for pair in range(pairs):
        first = min(max(2 * pair - 1, 0), columns - 4)
        shift = 2 * pair - first
        if shift not in biases:
            near = jnp.abs(key_tile - query_tile - shift) <= 1
            base = jnp.where(near, 0.0, NEG)
            biases[shift] = (base + edge_ref[0], base, base + edge_ref[1])
    for half in range(2):
        lanes = slice(half * HD, half * HD + HD)
        wt = wt_ref[:, lanes]
        scores = []
        for pair in range(pairs):
            first = min(max(2 * pair - 1, 0), columns - 4)
            bias = biases[2 * pair - first]
            tokens = slice(2 * TILE * pair, 2 * TILE * (pair + 1))
            keys = slice(TILE * first, TILE * (first + 4))
            queries = [q[tokens, lanes] for q in q_refs]
            query = queries[0] if groups == 1 else jnp.concatenate(queries, axis=0)
            raw = dot(query, jnp.concatenate([k[keys, lanes] for k in k_refs], axis=0), NT)
            scores.append([raw[:, span * i : span * (i + 1)] + bias[i] for i in range(3)])
        tops = [jnp.max(functools.reduce(jnp.maximum, s), axis=1, keepdims=True) for s in scores]
        weights = [[jnp.exp2((x - top) * FACTOR) for x in s] for s, top in zip(scores, tops)]
        totals = [jnp.sum(sum(w), axis=1, keepdims=True) for w in weights]
        mixed = []
        for pair, weight in enumerate(weights):
            first = min(max(2 * pair - 1, 0), columns - 4)
            keys = slice(TILE * first, TILE * (first + 4))
            rounded = jnp.concatenate([w.astype(jnp.bfloat16) for w in weight], axis=1)
            mixed.append(dot(rounded, jnp.concatenate([v[keys, lanes] for v in v_refs], axis=0), NN))
        mixed = [(m * (1.0 / total)).astype(jnp.bfloat16) for m, total in zip(mixed, totals)]
        projected = [dot(wt, m, NT) for m in mixed]
        for pair in range(pairs):
            tokens = slice(2 * TILE * pair, 2 * TILE * (pair + 1))
            lse = tops[pair] * FACTOR + jnp.log2(totals[pair])
            for g in range(groups):
                part = slice(2 * TILE * g, 2 * TILE * (g + 1))
                p_refs[g][PATCH * half : PATCH * (half + 1), tokens] = projected[pair][:, part]
                held = acc_refs[g][tokens, :]
                mark = lane_iota(held.shape) == 2 * step + half
                acc_refs[g][tokens, :] = jnp.where(mark, lse[part], held)

    @pl.when(step == pl.num_programs(0) - 1)
    def _():
        for g in range(groups):
            l_refs[g][...] = jnp.transpose(acc_refs[g][...])[:LSE_ROWS, :]


def window_attention(edge, queries, query_block, keys, values, wt, columns, after=()):
    groups = len(queries)
    tokens = columns * TILE
    inner = wt.shape[1]
    steps = inner // (2 * HD)

    def block(row):
        return pl.BlockSpec((tokens, 2 * HD), lambda i, row=row: (row, i))

    specs = [pl.BlockSpec(memory_space=pltpu.SMEM)]
    specs += [block(query_block) for _ in queries]
    specs += [block(row) for _, row in keys] + [block(row) for _, row in values]
    specs += [pl.BlockSpec((PATCH, 2 * HD), lambda i: (0, i))]
    specs += [pl.BlockSpec(memory_space=pl.ANY)] * len(after)
    operands = [edge, *queries, *[a for a, _ in keys], *[a for a, _ in values], wt, *after]
    heads = inner // HD
    flops = 2 * groups * tokens * heads * 12 * TILE * HD * 2
    out = pl.pallas_call(
        functools.partial(window_kernel, groups, columns),
        grid=(steps,),
        in_specs=specs,
        out_specs=[pl.BlockSpec((2 * PATCH, tokens), lambda i: (i, 0))] * groups
        + [pl.BlockSpec((LSE_ROWS, tokens), lambda i: (0, 0))] * groups,
        out_shape=[jax.ShapeDtypeStruct((heads * PATCH, tokens), jnp.float32)] * groups
        + [jax.ShapeDtypeStruct((LSE_ROWS, tokens), jnp.float32)] * groups,
        scratch_shapes=[pltpu.VMEM((tokens, 128), jnp.float32)] * groups,
        compiler_params=pltpu.CompilerParams(vmem_limit_bytes=56 * MIB),
        cost_estimate=pl.CostEstimate(flops=1, bytes_accessed=1, transcendentals=0),
    )(*operands)
    return out[:groups], out[groups:]


def far_kernel(per_step, heads, index_ref, query_ref, key_ref, value_ref, wbd_ref, *refs):
    out_ref, lse_ref = refs[-2:]
    step = pl.program_id(0)
    upper = lax.broadcasted_iota(jnp.int32, (2 * TILE, 2 * HD), 0) // TILE
    right = lane_iota((2 * TILE, 2 * HD)) // HD
    own_half = upper == right
    lane = lane_iota((TILE, 128))
    slots = range(per_step)
    pairs = range(heads // 2)
    starts = [pl.multiple_of(index_ref[step * per_step + s] * TILE, TILE) for s in slots]
    scores = []
    for s in slots:
        parts = []
        for j in pairs:
            lanes = slice(2 * j * HD, 2 * (j + 1) * HD)
            query = query_ref[s * TILE : (s + 1) * TILE, lanes]
            stacked = jnp.concatenate([query, query], axis=0)
            stacked = jnp.where(own_half, stacked, jnp.zeros_like(stacked))
            parts.append(dot(stacked, key_ref[pl.ds(starts[s], TILE), lanes], NT))
        scores.append(jnp.concatenate(parts, axis=0))
    tops = [jnp.max(x, axis=1, keepdims=True) for x in scores]
    weights = [jnp.exp2((x - top) * FACTOR) for x, top in zip(scores, tops)]
    totals = [jnp.sum(w, axis=1, keepdims=True) for w in weights]
    rounded = [w.astype(jnp.bfloat16) for w in weights]
    inverse = [1.0 / total for total in totals]
    lses = [top * FACTOR + jnp.log2(total) for top, total in zip(tops, totals)]
    mixed = []
    for s in slots:
        for j in pairs:
            lanes = slice(2 * j * HD, 2 * (j + 1) * HD)
            pair = slice(2 * j * TILE, 2 * (j + 1) * TILE)
            both = dot(rounded[s][pair], value_ref[pl.ds(starts[s], TILE), lanes], NN) * inverse[s][pair]
            mixed.append(jnp.concatenate([both[:TILE, :HD], both[TILE:, HD:]], axis=1).astype(jnp.bfloat16))
    for j in pairs:
        lanes = slice(2 * j * PATCH, 2 * (j + 1) * PATCH)
        stacked = jnp.concatenate([mixed[s * (heads // 2) + j] for s in slots], axis=0)
        out_ref[:, lanes] = dot(stacked, wbd_ref[:, lanes], NN).astype(jnp.bfloat16)
    sums = []
    for s in slots:
        column = jnp.zeros((TILE, 128), jnp.float32)
        for head in range(heads):
            column = jnp.where(lane == head, lses[s][head * TILE : (head + 1) * TILE], column)
        sums.append(column)
    turned = jnp.transpose(jnp.concatenate(sums, axis=0))[:LSE_ROWS]
    for o in range(per_step // SLOTS):
        lse_ref[o] = turned[:, o * SLOTS * TILE : (o + 1) * SLOTS * TILE]


def far_attention(index, received, key, value, wbd, after):
    count = index.shape[0]
    inner = key.shape[1]
    heads = inner // HD
    per_step = 4
    width = heads * PATCH
    return pl.pallas_call(
        functools.partial(far_kernel, per_step, heads),
        grid_spec=pltpu.PrefetchScalarGridSpec(
            num_scalar_prefetch=1,
            grid=(count // per_step,),
            in_specs=[
                pl.BlockSpec((per_step * TILE, inner), lambda i, _: (i, 0)),
                pl.BlockSpec(key.shape, lambda i, _: (0, 0)),
                pl.BlockSpec(value.shape, lambda i, _: (0, 0)),
                pl.BlockSpec(wbd.shape, lambda i, _: (0, 0)),
            ]
            + [pl.BlockSpec(memory_space=pl.ANY)] * len(after),
            out_specs=[
                pl.BlockSpec((per_step * TILE, width), lambda i, _: (i, 0)),
                pl.BlockSpec((per_step // SLOTS, LSE_ROWS, SLOTS * TILE), lambda i, _: (i, 0, 0)),
            ],
        ),
        out_shape=[
            jax.ShapeDtypeStruct((count * TILE, width), jnp.bfloat16),
            jax.ShapeDtypeStruct((count // SLOTS, LSE_ROWS, SLOTS * TILE), jnp.float32),
        ],
        compiler_params=pltpu.CompilerParams(vmem_limit_bytes=56 * MIB),
        cost_estimate=pl.CostEstimate(flops=1, bytes_accessed=1, transcendentals=0),
    )(index, received, key, value, wbd, *after)


def log_sum(*parts):
    top = functools.reduce(jnp.maximum, parts)
    return top + jnp.log2(sum(jnp.exp2(p - top) for p in parts))


def weighted_sum(weights, projected, heads):
    return sum(weights[h : h + 1, :] * projected[PATCH * h : PATCH * (h + 1), :] for h in range(heads))


def base_kernel(row_tiles, slot_ref, far_ref, *refs):
    own_refs = refs[:-2]
    far_out, base_out = refs[-2:]
    for r, own_ref in enumerate(own_refs):
        for c in range(row_tiles):
            slot = slot_ref[r * row_tiles + c]
            held = far_ref[slot // SLOTS]
            far = jnp.where(slot % SLOTS == 0, held[:, :TILE], held[:, TILE:])
            lanes = slice((r * row_tiles + c) * TILE, (r * row_tiles + c + 1) * TILE)
            far_out[:, lanes] = far
            base_out[:, lanes] = log_sum(own_ref[:, c * TILE : (c + 1) * TILE], far)


def tie(value, after):
    def kernel(*refs):
        pass

    anywhere = pl.BlockSpec(memory_space=pl.ANY)
    return pl.pallas_call(
        kernel,
        in_specs=[anywhere] * (1 + len(after)),
        out_specs=anywhere,
        out_shape=jax.ShapeDtypeStruct(value.shape, value.dtype),
        input_output_aliases={0: 0},
    )(value, *after)


def merge_kernel(heads, chunks, base, far_l, far_p, *refs):
    out = refs[-1]
    for c in range(chunks):
        p, l = refs[2 * c : 2 * c + 2]
        tokens = l.shape[1]
        cols = slice(c * tokens, (c + 1) * tokens)
        far = jnp.transpose(far_p[cols, :].astype(jnp.float32))
        own_weight = jnp.exp2(l[...] - base[:, cols])
        far_weight = jnp.exp2(far_l[:, cols] - base[:, cols])
        for h in range(heads):
            rows = slice(PATCH * h, PATCH * (h + 1))
            out[rows, cols] = own_weight[h : h + 1, :] * p[rows, :] + far_weight[h : h + 1, :] * far[rows, :]


def whole(kernel, out_shape, cost, *operands, smem=0, after=()):
    specs = [pl.BlockSpec(memory_space=pltpu.SMEM)] * smem
    specs += [pl.BlockSpec(memory_space=pltpu.VMEM)] * (len(operands) - smem)
    specs += [pl.BlockSpec(memory_space=pl.ANY)] * len(after)
    return pl.pallas_call(
        kernel,
        in_specs=specs,
        out_specs=jax.tree.map(lambda _: pl.BlockSpec(memory_space=pltpu.VMEM), out_shape),
        out_shape=out_shape,
        compiler_params=pltpu.CompilerParams(vmem_limit_bytes=56 * MIB),
        cost_estimate=pl.CostEstimate(flops=1, bytes_accessed=1, transcendentals=0),
    )(*operands, *after)


def scale_kernel(heads, chunks, flags, other, *refs):
    up_out, down_out = refs[-2:]
    for side, out in enumerate((up_out, down_out)):
        base = refs[2 * chunks * 2 + side]
        for c in range(chunks):
            p, l = refs[2 * (chunks * side + c) : 2 * (chunks * side + c) + 2]
            tokens = l.shape[1]
            cols = slice(c * tokens, (c + 1) * tokens)
            lse = l[...]
            weights = jnp.exp2(lse - log_sum(lse, base[:, cols], other[:, cols] + flags[side]))
            out[:PATCH, cols] = weighted_sum(weights, p, heads)
            out[PATCH:, cols] = lse


def final_kernel(heads, scalars, p, l, above, below, target, error_out, sum_out):
    lse = l[...]
    sums = log_sum(lse, above[PATCH:, :] + scalars[1], below[PATCH:, :] + scalars[2])
    out = weighted_sum(jnp.exp2(lse - sums), p, heads) + above[:PATCH, :] + below[:PATCH, :]
    error = jnp.transpose(out) - target[...].astype(jnp.float32)
    error_out[...] = (scalars[0] * error).astype(jnp.bfloat16)
    sum_out[...] = jnp.broadcast_to(jnp.sum(error * error, keepdims=True), sum_out.shape)


def body(
    query_tokens,
    key_tokens,
    value_tokens,
    head_weight,
    target_noise,
    far_owner,
    far_offset,
    timestep,
    labels,
):
    _, _, rows_dev, columns, tile_len, inner = query_tokens.shape
    tiles = rows_dev * columns
    heads = inner // HD
    row_tokens = columns * tile_len
    tokens = rows_dev * row_tokens
    pairs_n, frames_n, height_n = (lax.axis_size(a) for a in ("pair", "tm", "height"))
    frame = lax.axis_index("tm")
    height = lax.axis_index("height")

    up_frames = [(i, i + 1) for i in range(frames_n - 1)]
    down_frames = [(i + 1, i) for i in range(frames_n - 1)]
    up_rows = [(i, i + 1) for i in range(height_n - 1)]
    down_rows = [(i + 1, i) for i in range(height_n - 1)]

    query = query_tokens.reshape(tokens, inner)
    key = key_tokens.reshape(tokens, inner)
    value = value_tokens.reshape(tokens, inner)

    last = jnp.concatenate([key[row_tokens:], value[row_tokens:]], axis=0)
    initial = jnp.concatenate([key[:row_tokens], value[:row_tokens]], axis=0)
    halo_before = lax.ppermute(last, "height", up_rows)
    halo_after = lax.ppermute(initial, "height", down_rows)

    owners = far_owner.reshape(tiles)
    offsets = far_offset.reshape(tiles)
    ids = jnp.arange(tiles)
    earlier = (ids[:, None] > ids[None, :]) & (owners[:, None] == owners[None, :])
    slot = owners * SLOTS + jnp.sum(earlier.astype(jnp.int32), axis=1)
    slot_count = height_n * SLOTS
    chosen = slot[:, None] == jnp.arange(slot_count)[None, :]
    source = jnp.sum(jnp.where(chosen, ids[:, None], 0), axis=0)
    marks = jnp.broadcast_to(offsets.astype(jnp.bfloat16)[:, None, None], (tiles, tile_len, 128))
    payload = jnp.concatenate([query.reshape(tiles, tile_len, inner), marks], axis=2)[source]
    payload = tie(payload, [halo_before, halo_after])
    received = lax.all_to_all(payload, "height", split_axis=0, concat_axis=0, tiled=True)

    from_below = []
    from_above = []
    for r in range(rows_dev):
        part = tie(query[r * row_tokens : (r + 1) * row_tokens], [halo_before, halo_after])
        from_below.append(lax.ppermute(part, "tm", up_frames))
        from_above.append(lax.ppermute(part, "tm", down_frames))

    wt = jnp.transpose(head_weight)
    paired = head_weight.reshape(heads // 2, 2, HD, PATCH)
    wbd = jnp.zeros((2, HD, heads // 2, 2, PATCH), head_weight.dtype)
    for half in range(2):
        wbd = wbd.at[half, :, :, half, :].set(jnp.transpose(paired[:, half], (1, 0, 2)))
    wbd = wbd.reshape(2 * HD, heads * PATCH)

    first_edge = jnp.where(height == 0, NEG, 0.0).astype(jnp.float32)
    last_edge = jnp.where(height == height_n - 1, NEG, 0.0).astype(jnp.float32)
    zero = jnp.zeros((), jnp.float32)

    def attend(r, queries, block, first=()):
        before = (halo_before, 0, halo_before, 1) if r == 0 else (key, r - 1, value, r - 1)
        after = (halo_after, 0, halo_after, 1) if r == rows_dev - 1 else (key, r + 1, value, r + 1)
        edge = jnp.stack([first_edge if r == 0 else zero, last_edge if r == rows_dev - 1 else zero])
        keys = [before[:2], (key, r), after[:2]]
        values = [before[2:], (value, r), after[2:]]
        return window_attention(edge, queries, block, keys, values, wt, columns, first)

    own = []
    for r in range(rows_dev):
        (p,), (l,) = attend(r, [query], r)
        own.append((p, l))

    index = received[:, 0, inner].astype(jnp.int32)
    received = received.reshape(slot_count * tile_len, inner + 128)
    far_p, far_l = far_attention(index, received, key, value, wbd, [l for _, l in own])
    far_l = lax.all_to_all(far_l, "height", split_axis=0, concat_axis=0, tiled=True)
    flat = jax.ShapeDtypeStruct((LSE_ROWS, tokens), jnp.float32)
    far_l, base_lse = whole(
        functools.partial(base_kernel, columns), [flat, flat], 0, slot, far_l, *[l for _, l in own], smem=1
    )
    base_below = lax.ppermute(base_lse, "tm", up_frames)
    base_above = lax.ppermute(base_lse, "tm", down_frames)

    swap = [(i, i + 2) for i in range(frames_n - 2)] + [(i + 2, i) for i in range(frames_n - 2)]
    low = frame < frames_n - 2
    ups = []
    downs = []
    for r in range(rows_dev):
        (pd, pu), (ld, lu) = attend(r, [from_below[r], from_above[r]], 0)
        ups.append((pu, lu))
        downs.append((pd, ld))
    width = far_p.shape[1]
    far_p = tie(far_p, [ups[0][1], from_below[-1], from_above[-1]])
    far_p = lax.all_to_all(
        far_p.reshape(slot_count, tile_len, width), "height", split_axis=0, concat_axis=0, tiled=True
    )
    base_p = whole(
        functools.partial(merge_kernel, heads, rows_dev),
        jax.ShapeDtypeStruct((width, tokens), jnp.float32),
        0,
        base_lse,
        far_l,
        far_p[slot].reshape(tokens, width),
        *[a for part in own for a in part],
    )
    lse_u = jnp.concatenate([l for _, l in ups], axis=1)
    lse_d = jnp.concatenate([l for _, l in downs], axis=1)
    other = lax.ppermute(jnp.where(low, lse_u, lse_d), "tm", swap)
    flags = jnp.where(low, jnp.array([0.0, NEG]), jnp.array([NEG, 0.0])).astype(jnp.float32)
    shape = jax.ShapeDtypeStruct((PATCH + LSE_ROWS, tokens), jnp.float32)
    to_above, to_below = whole(
        functools.partial(scale_kernel, heads, rows_dev),
        [shape, shape],
        0,
        flags,
        other,
        *[a for part in ups + downs for a in part],
        base_above,
        base_below,
        smem=1,
    )
    got_below = lax.ppermute(to_above, "tm", up_frames)
    got_above = lax.ppermute(to_below, "tm", down_frames)

    pair = lax.axis_index("pair")
    pair_slot = pair // 2
    step_weight = 0.5 + (timestep[pair_slot].astype(jnp.float32) + 1.0) / 1000.0
    no_above = jnp.where(frame == frames_n - 1, NEG, 0.0).astype(jnp.float32)
    no_below = jnp.where(frame == 0, NEG, 0.0).astype(jnp.float32)
    scalars = jnp.stack([jnp.sqrt(step_weight), no_above, no_below])
    error, squares = whole(
        functools.partial(final_kernel, heads),
        [jax.ShapeDtypeStruct((tokens, PATCH), jnp.bfloat16), jax.ShapeDtypeStruct((pairs_n * frames_n * height_n, 128), jnp.float32)],
        1 << 22,
        scalars,
        base_p,
        base_lse,
        got_above,
        got_below,
        target_noise.reshape(tokens, PATCH),
        smem=1,
    )
    weighted_error = error.reshape(target_noise.shape)

    gathered = lax.all_to_all(squares, ("pair", "tm", "height"), split_axis=0, concat_axis=0, tiled=True)
    sums = jnp.sum(gathered.reshape(pairs_n, frames_n * height_n, 128)[:, :, 0], axis=1)
    count = frames_n * height_n * tokens * PATCH
    mine = sums[pair]
    partner = sums[pair ^ 1]
    clip_loss = step_weight * mine / count
    partner_loss = step_weight * partner / count
    difference = jnp.where(pair % 2 == 1, clip_loss - partner_loss, partner_loss - clip_loss)
    strength = 2.0 * labels[pair_slot].astype(jnp.float32) / RATERS - 1.0
    return (weighted_error, clip_loss.reshape(1), (strength * difference).reshape(1))


def solution(mesh):
    placed = (
        P("pair", "tm", "height", None, None, None),
        P("pair", "tm", "height", None, None, None),
        P("pair", "tm", "height", None, None, None),
        P(),
        P("pair", "tm", "height", None, None, None),
        P("pair", "tm", "height", None, None),
        P("pair", "tm", "height", None, None),
        P(),
        P(),
    )
    return jax.shard_map(
        body,
        mesh=mesh,
        in_specs=placed,
        out_specs=(P("pair", "tm", "height", None, None, None), P("pair"), P("pair")),
        check_vma=False,
    )
```

```python
import functools
import math

import jax
import jax.numpy as jnp
from jax import lax
from jax.experimental import pallas as pl
from jax.experimental.pallas import tpu as pltpu
from jax.sharding import PartitionSpec as P

HEADS = 12
HD = 128
PATCH = 64
TILE = 32
RATERS = 100
SLOTS = 2
NEG = -1e30
FACTOR = math.log2(math.e) / math.sqrt(HD)
LSE_ROWS = 16
MIB = 1 << 20

NT = (((1,), (1,)), ((), ()))
NN = (((1,), (0,)), ((), ()))


def dot(a, b, dims):
    return lax.dot_general(a, b, dims, preferred_element_type=jnp.float32)


def lane_iota(shape):
    return lax.broadcasted_iota(jnp.int32, shape, 1)


def window_kernel(groups, columns, edge_ref, *refs):
    q_refs = refs[:groups]
    k_refs = refs[groups : groups + 3]
    v_refs = refs[groups + 3 : groups + 6]
    wt_ref = refs[groups + 6]
    p_refs = refs[-3 * groups : -2 * groups]
    l_refs = refs[-2 * groups : -groups]
    acc_refs = refs[-groups:]
    step = pl.program_id(0)
    span = 4 * TILE
    rows = 2 * TILE * groups

    @pl.when(step == 0)
    def _():
        for acc in acc_refs:
            acc[...] = jnp.zeros_like(acc)

    key_tile = lane_iota((rows, span)) // TILE
    query_tile = (lax.broadcasted_iota(jnp.int32, (rows, span), 0) // TILE) % 2
    biases = {}
    pairs = columns // 2
    for pair in range(pairs):
        first = min(max(2 * pair - 1, 0), columns - 4)
        shift = 2 * pair - first
        if shift not in biases:
            near = jnp.abs(key_tile - query_tile - shift) <= 1
            base = jnp.where(near, 0.0, NEG)
            biases[shift] = (base + edge_ref[0], base, base + edge_ref[1])
    for half in range(2):
        lanes = slice(half * HD, half * HD + HD)
        wt = wt_ref[:, lanes]
        scores = []
        for pair in range(pairs):
            first = min(max(2 * pair - 1, 0), columns - 4)
            bias = biases[2 * pair - first]
            tokens = slice(2 * TILE * pair, 2 * TILE * (pair + 1))
            keys = slice(TILE * first, TILE * (first + 4))
            queries = [q[tokens, lanes] for q in q_refs]
            query = queries[0] if groups == 1 else jnp.concatenate(queries, axis=0)
            raw = dot(query, jnp.concatenate([k[keys, lanes] for k in k_refs], axis=0), NT)
            scores.append([raw[:, span * i : span * (i + 1)] + bias[i] for i in range(3)])
        tops = [jnp.max(functools.reduce(jnp.maximum, s), axis=1, keepdims=True) for s in scores]
        weights = [[jnp.exp2((x - top) * FACTOR) for x in s] for s, top in zip(scores, tops)]
        totals = [jnp.sum(sum(w), axis=1, keepdims=True) for w in weights]
        mixed = []
        for pair, weight in enumerate(weights):
            first = min(max(2 * pair - 1, 0), columns - 4)
            keys = slice(TILE * first, TILE * (first + 4))
            rounded = jnp.concatenate([w.astype(jnp.bfloat16) for w in weight], axis=1)
            mixed.append(dot(rounded, jnp.concatenate([v[keys, lanes] for v in v_refs], axis=0), NN))
        mixed = [(m * (1.0 / total)).astype(jnp.bfloat16) for m, total in zip(mixed, totals)]
        projected = [dot(wt, m, NT) for m in mixed]
        for pair in range(pairs):
            tokens = slice(2 * TILE * pair, 2 * TILE * (pair + 1))
            lse = tops[pair] * FACTOR + jnp.log2(totals[pair])
            for g in range(groups):
                part = slice(2 * TILE * g, 2 * TILE * (g + 1))
                p_refs[g][PATCH * half : PATCH * (half + 1), tokens] = projected[pair][:, part]
                held = acc_refs[g][tokens, :]
                mark = lane_iota(held.shape) == 2 * step + half
                acc_refs[g][tokens, :] = jnp.where(mark, lse[part], held)

    @pl.when(step == pl.num_programs(0) - 1)
    def _():
        for g in range(groups):
            l_refs[g][...] = jnp.transpose(acc_refs[g][...])[:LSE_ROWS, :]


def window_attention(edge, queries, query_block, keys, values, wt, columns, after=()):
    groups = len(queries)
    tokens = columns * TILE
    inner = wt.shape[1]
    steps = inner // (2 * HD)

    def block(row):
        return pl.BlockSpec((tokens, 2 * HD), lambda i, row=row: (row, i))

    specs = [pl.BlockSpec(memory_space=pltpu.SMEM)]
    specs += [block(query_block) for _ in queries]
    specs += [block(row) for _, row in keys] + [block(row) for _, row in values]
    specs += [pl.BlockSpec((PATCH, 2 * HD), lambda i: (0, i))]
    specs += [pl.BlockSpec(memory_space=pl.ANY)] * len(after)
    operands = [edge, *queries, *[a for a, _ in keys], *[a for a, _ in values], wt, *after]
    heads = inner // HD
    flops = 2 * groups * tokens * heads * 12 * TILE * HD * 2
    out = pl.pallas_call(
        functools.partial(window_kernel, groups, columns),
        grid=(steps,),
        in_specs=specs,
        out_specs=[pl.BlockSpec((2 * PATCH, tokens), lambda i: (i, 0))] * groups
        + [pl.BlockSpec((LSE_ROWS, tokens), lambda i: (0, 0))] * groups,
        out_shape=[jax.ShapeDtypeStruct((heads * PATCH, tokens), jnp.float32)] * groups
        + [jax.ShapeDtypeStruct((LSE_ROWS, tokens), jnp.float32)] * groups,
        scratch_shapes=[pltpu.VMEM((tokens, 128), jnp.float32)] * groups,
        compiler_params=pltpu.CompilerParams(vmem_limit_bytes=56 * MIB),
        cost_estimate=pl.CostEstimate(flops=1, bytes_accessed=1, transcendentals=0),
    )(*operands)
    return out[:groups], out[groups:]


def far_kernel(per_step, heads, index_ref, query_ref, key_ref, value_ref, wbd_ref, *refs):
    out_ref, lse_ref = refs[-2:]
    step = pl.program_id(0)
    upper = lax.broadcasted_iota(jnp.int32, (2 * TILE, 2 * HD), 0) // TILE
    right = lane_iota((2 * TILE, 2 * HD)) // HD
    own_half = upper == right
    lane = lane_iota((TILE, 128))
    slots = range(per_step)
    pairs = range(heads // 2)
    starts = [pl.multiple_of(index_ref[step * per_step + s] * TILE, TILE) for s in slots]
    scores = []
    for s in slots:
        parts = []
        for j in pairs:
            lanes = slice(2 * j * HD, 2 * (j + 1) * HD)
            query = query_ref[s * TILE : (s + 1) * TILE, lanes]
            stacked = jnp.concatenate([query, query], axis=0)
            stacked = jnp.where(own_half, stacked, jnp.zeros_like(stacked))
            parts.append(dot(stacked, key_ref[pl.ds(starts[s], TILE), lanes], NT))
        scores.append(jnp.concatenate(parts, axis=0))
    tops = [jnp.max(x, axis=1, keepdims=True) for x in scores]
    weights = [jnp.exp2((x - top) * FACTOR) for x, top in zip(scores, tops)]
    totals = [jnp.sum(w, axis=1, keepdims=True) for w in weights]
    rounded = [w.astype(jnp.bfloat16) for w in weights]
    inverse = [1.0 / total for total in totals]
    lses = [top * FACTOR + jnp.log2(total) for top, total in zip(tops, totals)]
    mixed = []
    for s in slots:
        for j in pairs:
            lanes = slice(2 * j * HD, 2 * (j + 1) * HD)
            pair = slice(2 * j * TILE, 2 * (j + 1) * TILE)
            both = dot(rounded[s][pair], value_ref[pl.ds(starts[s], TILE), lanes], NN) * inverse[s][pair]
            mixed.append(jnp.concatenate([both[:TILE, :HD], both[TILE:, HD:]], axis=1).astype(jnp.bfloat16))
    for j in pairs:
        lanes = slice(2 * j * PATCH, 2 * (j + 1) * PATCH)
        stacked = jnp.concatenate([mixed[s * (heads // 2) + j] for s in slots], axis=0)
        out_ref[:, lanes] = dot(stacked, wbd_ref[:, lanes], NN).astype(jnp.bfloat16)
    sums = []
    for s in slots:
        column = jnp.zeros((TILE, 128), jnp.float32)
        for head in range(heads):
            column = jnp.where(lane == head, lses[s][head * TILE : (head + 1) * TILE], column)
        sums.append(column)
    turned = jnp.transpose(jnp.concatenate(sums, axis=0))[:LSE_ROWS]
    for o in range(per_step // SLOTS):
        lse_ref[o] = turned[:, o * SLOTS * TILE : (o + 1) * SLOTS * TILE]


def far_attention(index, received, key, value, wbd, after):
    count = index.shape[0]
    inner = key.shape[1]
    heads = inner // HD
    per_step = 4
    width = heads * PATCH
    return pl.pallas_call(
        functools.partial(far_kernel, per_step, heads),
        grid_spec=pltpu.PrefetchScalarGridSpec(
            num_scalar_prefetch=1,
            grid=(count // per_step,),
            in_specs=[
                pl.BlockSpec((per_step * TILE, inner), lambda i, _: (i, 0)),
                pl.BlockSpec(key.shape, lambda i, _: (0, 0)),
                pl.BlockSpec(value.shape, lambda i, _: (0, 0)),
                pl.BlockSpec(wbd.shape, lambda i, _: (0, 0)),
            ]
            + [pl.BlockSpec(memory_space=pl.ANY)] * len(after),
            out_specs=[
                pl.BlockSpec((per_step * TILE, width), lambda i, _: (i, 0)),
                pl.BlockSpec((per_step // SLOTS, LSE_ROWS, SLOTS * TILE), lambda i, _: (i, 0, 0)),
            ],
        ),
        out_shape=[
            jax.ShapeDtypeStruct((count * TILE, width), jnp.bfloat16),
            jax.ShapeDtypeStruct((count // SLOTS, LSE_ROWS, SLOTS * TILE), jnp.float32),
        ],
        compiler_params=pltpu.CompilerParams(vmem_limit_bytes=56 * MIB),
        cost_estimate=pl.CostEstimate(flops=1, bytes_accessed=1, transcendentals=0),
    )(index, received, key, value, wbd, *after)


def log_sum(*parts):
    top = functools.reduce(jnp.maximum, parts)
    return top + jnp.log2(sum(jnp.exp2(p - top) for p in parts))


def weighted_sum(weights, projected, heads):
    return sum(weights[h : h + 1, :] * projected[PATCH * h : PATCH * (h + 1), :] for h in range(heads))


def base_kernel(row_tiles, slot_ref, far_ref, *refs):
    own_refs = refs[:-2]
    far_out, base_out = refs[-2:]
    for r, own_ref in enumerate(own_refs):
        for c in range(row_tiles):
            slot = slot_ref[r * row_tiles + c]
            held = far_ref[slot // SLOTS]
            far = jnp.where(slot % SLOTS == 0, held[:, :TILE], held[:, TILE:])
            lanes = slice((r * row_tiles + c) * TILE, (r * row_tiles + c + 1) * TILE)
            far_out[:, lanes] = far
            base_out[:, lanes] = log_sum(own_ref[:, c * TILE : (c + 1) * TILE], far)


def tie(value, after):
    def kernel(*refs):
        pass

    anywhere = pl.BlockSpec(memory_space=pl.ANY)
    return pl.pallas_call(
        kernel,
        in_specs=[anywhere] * (1 + len(after)),
        out_specs=anywhere,
        out_shape=jax.ShapeDtypeStruct(value.shape, value.dtype),
        input_output_aliases={0: 0},
    )(value, *after)


def merge_kernel(heads, chunks, base, far_l, far_p, *refs):
    out = refs[-1]
    for c in range(chunks):
        p, l = refs[2 * c : 2 * c + 2]
        tokens = l.shape[1]
        cols = slice(c * tokens, (c + 1) * tokens)
        far = jnp.transpose(far_p[cols, :].astype(jnp.float32))
        own_weight = jnp.exp2(l[...] - base[:, cols])
        far_weight = jnp.exp2(far_l[:, cols] - base[:, cols])
        for h in range(heads):
            rows = slice(PATCH * h, PATCH * (h + 1))
            out[rows, cols] = own_weight[h : h + 1, :] * p[rows, :] + far_weight[h : h + 1, :] * far[rows, :]


def whole(kernel, out_shape, cost, *operands, smem=0, after=()):
    specs = [pl.BlockSpec(memory_space=pltpu.SMEM)] * smem
    specs += [pl.BlockSpec(memory_space=pltpu.VMEM)] * (len(operands) - smem)
    specs += [pl.BlockSpec(memory_space=pl.ANY)] * len(after)
    return pl.pallas_call(
        kernel,
        in_specs=specs,
        out_specs=jax.tree.map(lambda _: pl.BlockSpec(memory_space=pltpu.VMEM), out_shape),
        out_shape=out_shape,
        compiler_params=pltpu.CompilerParams(vmem_limit_bytes=56 * MIB),
        cost_estimate=pl.CostEstimate(flops=1, bytes_accessed=1, transcendentals=0),
    )(*operands, *after)


def scale_kernel(heads, chunks, flags, other, *refs):
    up_out, down_out = refs[-2:]
    for side, out in enumerate((up_out, down_out)):
        base = refs[2 * chunks * 2 + side]
        for c in range(chunks):
            p, l = refs[2 * (chunks * side + c) : 2 * (chunks * side + c) + 2]
            tokens = l.shape[1]
            cols = slice(c * tokens, (c + 1) * tokens)
            lse = l[...]
            weights = jnp.exp2(lse - log_sum(lse, base[:, cols], other[:, cols] + flags[side]))
            out[:PATCH, cols] = weighted_sum(weights, p, heads).astype(jnp.bfloat16)
            for i in range(3):
                part = lse.astype(jnp.bfloat16)
                out[PATCH + LSE_ROWS * i : PATCH + LSE_ROWS * (i + 1), cols] = part
                lse = lse - part.astype(jnp.float32)


def final_kernel(heads, scalars, p, l, above, below, target, error_out, sum_out):
    lse = l[...]
    parts = [message[...].astype(jnp.float32) for message in (above, below)]
    lses = [sum(m[PATCH + LSE_ROWS * i : PATCH + LSE_ROWS * (i + 1)] for i in range(3)) for m in parts]
    sums = log_sum(lse, lses[0] + scalars[1], lses[1] + scalars[2])
    out = weighted_sum(jnp.exp2(lse - sums), p, heads) + parts[0][:PATCH] + parts[1][:PATCH]
    error = jnp.transpose(out) - target[...].astype(jnp.float32)
    error_out[...] = (scalars[0] * error).astype(jnp.bfloat16)
    sum_out[...] = jnp.broadcast_to(jnp.sum(error * error, keepdims=True), sum_out.shape)


def body(
    query_tokens,
    key_tokens,
    value_tokens,
    head_weight,
    target_noise,
    far_owner,
    far_offset,
    timestep,
    labels,
):
    _, _, rows_dev, columns, tile_len, inner = query_tokens.shape
    tiles = rows_dev * columns
    heads = inner // HD
    row_tokens = columns * tile_len
    tokens = rows_dev * row_tokens
    pairs_n, frames_n, height_n = (lax.axis_size(a) for a in ("pair", "tm", "height"))
    frame = lax.axis_index("tm")
    height = lax.axis_index("height")

    up_frames = [(i, i + 1) for i in range(frames_n - 1)]
    down_frames = [(i + 1, i) for i in range(frames_n - 1)]
    up_rows = [(i, i + 1) for i in range(height_n - 1)]
    down_rows = [(i + 1, i) for i in range(height_n - 1)]

    query = query_tokens.reshape(tokens, inner)
    key = key_tokens.reshape(tokens, inner)
    value = value_tokens.reshape(tokens, inner)

    last = jnp.concatenate([key[row_tokens:], value[row_tokens:]], axis=0)
    initial = jnp.concatenate([key[:row_tokens], value[:row_tokens]], axis=0)
    halo_before = lax.ppermute(last, "height", up_rows)
    halo_after = lax.ppermute(initial, "height", down_rows)

    owners = far_owner.reshape(tiles)
    offsets = far_offset.reshape(tiles)
    ids = jnp.arange(tiles)
    earlier = (ids[:, None] > ids[None, :]) & (owners[:, None] == owners[None, :])
    slot = owners * SLOTS + jnp.sum(earlier.astype(jnp.int32), axis=1)
    slot_count = height_n * SLOTS
    chosen = slot[:, None] == jnp.arange(slot_count)[None, :]
    source = jnp.sum(jnp.where(chosen, ids[:, None], 0), axis=0)
    marks = jnp.broadcast_to(offsets.astype(jnp.bfloat16)[:, None, None], (tiles, tile_len, 128))
    payload = jnp.concatenate([query.reshape(tiles, tile_len, inner), marks], axis=2)[source]
    payload = tie(payload, [halo_before, halo_after])
    received = lax.all_to_all(payload, "height", split_axis=0, concat_axis=0, tiled=True)

    from_below = []
    from_above = []
    for r in range(rows_dev):
        part = tie(query[r * row_tokens : (r + 1) * row_tokens], [halo_before, halo_after])
        from_below.append(lax.ppermute(part, "tm", up_frames))
        from_above.append(lax.ppermute(part, "tm", down_frames))

    wt = jnp.transpose(head_weight)
    paired = head_weight.reshape(heads // 2, 2, HD, PATCH)
    wbd = jnp.zeros((2, HD, heads // 2, 2, PATCH), head_weight.dtype)
    for half in range(2):
        wbd = wbd.at[half, :, :, half, :].set(jnp.transpose(paired[:, half], (1, 0, 2)))
    wbd = wbd.reshape(2 * HD, heads * PATCH)

    first_edge = jnp.where(height == 0, NEG, 0.0).astype(jnp.float32)
    last_edge = jnp.where(height == height_n - 1, NEG, 0.0).astype(jnp.float32)
    zero = jnp.zeros((), jnp.float32)

    def attend(r, queries, block, first=()):
        before = (halo_before, 0, halo_before, 1) if r == 0 else (key, r - 1, value, r - 1)
        after = (halo_after, 0, halo_after, 1) if r == rows_dev - 1 else (key, r + 1, value, r + 1)
        edge = jnp.stack([first_edge if r == 0 else zero, last_edge if r == rows_dev - 1 else zero])
        keys = [before[:2], (key, r), after[:2]]
        values = [before[2:], (value, r), after[2:]]
        return window_attention(edge, queries, block, keys, values, wt, columns, first)

    own = []
    for r in range(rows_dev):
        (p,), (l,) = attend(r, [query], r)
        own.append((p, l))

    index = received[:, 0, inner].astype(jnp.int32)
    received = received.reshape(slot_count * tile_len, inner + 128)
    far_p, far_l = far_attention(index, received, key, value, wbd, [l for _, l in own])
    far_l = lax.all_to_all(far_l, "height", split_axis=0, concat_axis=0, tiled=True)
    flat = jax.ShapeDtypeStruct((LSE_ROWS, tokens), jnp.float32)
    far_l, base_lse = whole(
        functools.partial(base_kernel, columns), [flat, flat], 0, slot, far_l, *[l for _, l in own], smem=1
    )
    base_below = lax.ppermute(base_lse, "tm", up_frames)
    base_above = lax.ppermute(base_lse, "tm", down_frames)

    swap = [(i, i + 2) for i in range(frames_n - 2)] + [(i + 2, i) for i in range(frames_n - 2)]
    low = frame < frames_n - 2
    ups = []
    downs = []
    for r in range(rows_dev):
        (pd, pu), (ld, lu) = attend(r, [from_below[r], from_above[r]], 0)
        ups.append((pu, lu))
        downs.append((pd, ld))
    width = far_p.shape[1]
    far_p = tie(far_p, [ups[0][1], from_below[-1], from_above[-1]])
    far_p = lax.all_to_all(
        far_p.reshape(slot_count, tile_len, width), "height", split_axis=0, concat_axis=0, tiled=True
    )
    base_p = whole(
        functools.partial(merge_kernel, heads, rows_dev),
        jax.ShapeDtypeStruct((width, tokens), jnp.float32),
        0,
        base_lse,
        far_l,
        far_p[slot].reshape(tokens, width),
        *[a for part in own for a in part],
    )
    lse_u = jnp.concatenate([l for _, l in ups], axis=1)
    lse_d = jnp.concatenate([l for _, l in downs], axis=1)
    other = lax.ppermute(jnp.where(low, lse_u, lse_d), "tm", swap)
    flags = jnp.where(low, jnp.array([0.0, NEG]), jnp.array([NEG, 0.0])).astype(jnp.float32)
    shape = jax.ShapeDtypeStruct((PATCH + 3 * LSE_ROWS, tokens), jnp.bfloat16)
    to_above, to_below = whole(
        functools.partial(scale_kernel, heads, rows_dev),
        [shape, shape],
        0,
        flags,
        other,
        *[a for part in ups + downs for a in part],
        base_above,
        base_below,
        smem=1,
    )
    got_below = lax.ppermute(to_above, "tm", up_frames)
    got_above = lax.ppermute(to_below, "tm", down_frames)

    pair = lax.axis_index("pair")
    pair_slot = pair // 2
    step_weight = 0.5 + (timestep[pair_slot].astype(jnp.float32) + 1.0) / 1000.0
    no_above = jnp.where(frame == frames_n - 1, NEG, 0.0).astype(jnp.float32)
    no_below = jnp.where(frame == 0, NEG, 0.0).astype(jnp.float32)
    scalars = jnp.stack([jnp.sqrt(step_weight), no_above, no_below])
    error, squares = whole(
        functools.partial(final_kernel, heads),
        [jax.ShapeDtypeStruct((tokens, PATCH), jnp.bfloat16), jax.ShapeDtypeStruct((pairs_n * frames_n * height_n, 128), jnp.float32)],
        1 << 22,
        scalars,
        base_p,
        base_lse,
        got_above,
        got_below,
        target_noise.reshape(tokens, PATCH),
        smem=1,
    )
    weighted_error = error.reshape(target_noise.shape)

    gathered = lax.all_to_all(squares, ("pair", "tm", "height"), split_axis=0, concat_axis=0, tiled=True)
    sums = jnp.sum(gathered.reshape(pairs_n, frames_n * height_n, 128)[:, :, 0], axis=1)
    count = frames_n * height_n * tokens * PATCH
    mine = sums[pair]
    partner = sums[pair ^ 1]
    clip_loss = step_weight * mine / count
    partner_loss = step_weight * partner / count
    difference = jnp.where(pair % 2 == 1, clip_loss - partner_loss, partner_loss - clip_loss)
    strength = 2.0 * labels[pair_slot].astype(jnp.float32) / RATERS - 1.0
    return (weighted_error, clip_loss.reshape(1), (strength * difference).reshape(1))


def solution(mesh):
    placed = (
        P("pair", "tm", "height", None, None, None),
        P("pair", "tm", "height", None, None, None),
        P("pair", "tm", "height", None, None, None),
        P(),
        P("pair", "tm", "height", None, None, None),
        P("pair", "tm", "height", None, None),
        P("pair", "tm", "height", None, None),
        P(),
        P(),
    )
    return jax.shard_map(
        body,
        mesh=mesh,
        in_specs=placed,
        out_specs=(P("pair", "tm", "height", None, None, None), P("pair"), P("pair")),
        check_vma=False,
    )
```
